32 devices in a mesh: seq: 8 (over z, x), head: 4 (over y, core).
Axes of the slice: x: 2, y: 2, z: 4, core: 2. Of those that a mesh axis runs over, the one named last changes fastest.
Arguments:
- queries: bfloat16 [8192, 1024], P('seq', 'head'), may hold values from -6 to 6
- keys: bfloat16 [8192, 512], P('seq', 'head'), may hold values from -6 to 6
- values: bfloat16 [8192, 512], P('seq', 'head'), may hold values from -6 to 6
- grad_out: bfloat16 [8192, 1024], P('seq', 'head'), may hold values from -6 to 6
- starts: int32 [64], P('seq'), may hold values 0 or 1
Outputs:
- grad_queries: bfloat16 [8192, 1024], P('seq', 'head')
- grad_keys: bfloat16 [8192, 512], P('seq', 'head')
- grad_values: bfloat16 [8192, 512], P('seq', 'head')
The draws below stay inside these ranges and needn't reach their ends.
Inputs may be any that keep to these rules, and one draw needn't show every extreme that they name: `starts`: blocks of 128 tokens, in storage order.
All inputs are finite; a program needn't handle non-finite values.
Results may differ from the reference program's by a relative error of at most 0.0087.
Values may be sent and summed in bfloat16 or wider, within the bound.
No kernel may reach another device: no remote copies, remote signals or barrier semaphores. Data moves between devices by JAX's collectives and lax.ppermute only.
A program may use at most 64 MiB of HBM per device.

```python
import jax
import jax.numpy as jnp
import numpy as np
from jax import lax

HEAD_SIZE = 128
WINDOW = 1024
QUERY_PER_KEY = 2
BLOCK = 128
KEY_VALUE_HEADS = 4
HQ = 8
PIECE_TOKENS = 512
PIECE_COUNT = 16
SEQUENCE_TOKENS = 8192
NBLK = 64
N_SEQ = 8


def draw_queries(key, part):
    return jnp.clip(jax.random.normal(jax.random.fold_in(key, 3), (SEQUENCE_TOKENS, HQ * HEAD_SIZE), jnp.float32), -4.0, 4.0).astype(jnp.bfloat16)


def draw_keys(key, part):
    return jnp.clip(jax.random.normal(jax.random.fold_in(key, 5), (SEQUENCE_TOKENS, KEY_VALUE_HEADS * HEAD_SIZE), jnp.float32), -4.0, 4.0).astype(jnp.bfloat16)


def touch_ends(result, own_key, smallest, high):
    spot = [jax.random.randint(jax.random.fold_in(own_key, axis), (), 0, length) for axis, length in enumerate(result.shape)]
    main_axis = result.shape.index(max(result.shape))
    next_to = spot[:main_axis] + [(spot[main_axis] + 1) % result.shape[main_axis]] + spot[main_axis + 1:]
    return result.at[tuple(spot)].set(smallest).at[tuple(next_to)].set(high)


def block_levels(stream_key, shape, split, least, largest):
    level = 1.0
    for position, shards_of in split:
        heights = jax.random.uniform(jax.random.fold_in(jax.random.fold_in(stream_key, 6), position), (shards_of,), jnp.float32, least / len(split), largest / len(split))
        level = level * jnp.repeat(jnp.exp(heights), shape[position] // shards_of).reshape((-1,) + (1,) * (len(shape) - 1 - position))
    return level


def scatter_about(own_key, shape, deviation, bound, cuts=(), kind=jnp.bfloat16):
    loudness = block_levels(own_key, shape, cuts, -0.22, 0.18) if cuts else 1.0
    values = jax.random.normal(own_key, shape, jnp.float32) * deviation * loudness
    return jnp.minimum(jnp.maximum(values, -bound), bound).astype(kind)


def setup_inputs(seed: int = 0) -> dict:
    splits = jax.random.split(jax.random.key(seed), 6)
    return {
        "queries": draw_queries(jax.random.fold_in(splits[5], 71), 0),
        "keys": draw_keys(jax.random.fold_in(splits[5], 71), 0),
        "values": scatter_about(splits[2], (SEQUENCE_TOKENS, KEY_VALUE_HEADS * HEAD_SIZE), 1.0, 6.0, ((0, 8), (1, 4))),
        "grad_out": scatter_about(splits[3], (SEQUENCE_TOKENS, HQ * HEAD_SIZE), 1.0, 6.0, ((0, 8), (1, 4))),
        "starts": touch_ends((jax.random.randint(splits[4], (NBLK,), 0, 8) < 1).astype(jnp.int32), jax.random.fold_in(splits[4], 1), 0, 1),
    }


query_scaling = 168.0 ** -0.5


def natural_places(n_seq):
    places = []
    for piece in range(2 * n_seq):
        if piece < n_seq:
            places.append(2 * piece)
        else:
            places.append(2 * (2 * n_seq - 1 - piece) + 1)
    return np.array(places, dtype=np.int32)


def reference(queries, keys, values, grad_out, starts):
    storage_lookup = natural_places(N_SEQ)
    inverse_order = np.argsort(storage_lookup).astype(np.int32)
    q_flat = queries.reshape(PIECE_COUNT, PIECE_TOKENS, HQ * HEAD_SIZE)[storage_lookup].reshape(SEQUENCE_TOKENS, HQ * HEAD_SIZE)
    g_flat = grad_out.reshape(PIECE_COUNT, PIECE_TOKENS, HQ * HEAD_SIZE)[storage_lookup].reshape(SEQUENCE_TOKENS, HQ * HEAD_SIZE)
    key_natural_order = keys.reshape(PIECE_COUNT, PIECE_TOKENS, KEY_VALUE_HEADS * HEAD_SIZE)[storage_lookup].reshape(SEQUENCE_TOKENS, KEY_VALUE_HEADS * HEAD_SIZE)
    value_natural_order = values.reshape(PIECE_COUNT, PIECE_TOKENS, KEY_VALUE_HEADS * HEAD_SIZE)[storage_lookup].reshape(SEQUENCE_TOKENS, KEY_VALUE_HEADS * HEAD_SIZE)
    start_nat = starts.reshape(PIECE_COUNT, PIECE_TOKENS // BLOCK)[storage_lookup].reshape(NBLK)
    doc_ids = jnp.cumsum(start_nat).astype(jnp.int32)
    token_doc = jnp.repeat(doc_ids, BLOCK)
    padding_rows = 2 * PIECE_TOKENS
    key_padded_rows = jnp.concatenate([jnp.zeros((padding_rows, KEY_VALUE_HEADS * HEAD_SIZE), keys.dtype), key_natural_order])
    value_padded_rows = jnp.concatenate([jnp.zeros((padding_rows, KEY_VALUE_HEADS * HEAD_SIZE), values.dtype), value_natural_order])
    doc_pad = jnp.concatenate([jnp.full((padding_rows,), -1, jnp.int32), token_doc])

    def one_piece(piece):
        begin = (piece * PIECE_TOKENS).astype(jnp.int32)
        query_rows_local = lax.dynamic_slice_in_dim(q_flat, begin, PIECE_TOKENS, 0)
        gradient_rows = lax.dynamic_slice_in_dim(g_flat, begin, PIECE_TOKENS, 0)
        key_rows_local = lax.dynamic_slice_in_dim(key_padded_rows, begin, 3 * PIECE_TOKENS, 0)
        value_rows_local = lax.dynamic_slice_in_dim(value_padded_rows, begin, 3 * PIECE_TOKENS, 0)
        d_rows = lax.dynamic_slice_in_dim(doc_pad, begin, 3 * PIECE_TOKENS, 0)
        key_pos = begin - 2 * PIECE_TOKENS + jnp.arange(3 * PIECE_TOKENS, dtype=jnp.int32)
        query_pos = begin + jnp.arange(PIECE_TOKENS, dtype=jnp.int32)
        offset = query_pos[:, None] - key_pos[None, :]
        query_doc = d_rows[2 * PIECE_TOKENS:]
        allowed = (offset >= 0) & (offset < WINDOW) & (key_pos[None, :] >= 0) & (query_doc[:, None] == d_rows[None, :])
        query_float = query_rows_local.astype(jnp.float32).reshape(PIECE_TOKENS, KEY_VALUE_HEADS, QUERY_PER_KEY, HEAD_SIZE)
        gradient_float = gradient_rows.astype(jnp.float32).reshape(PIECE_TOKENS, KEY_VALUE_HEADS, QUERY_PER_KEY, HEAD_SIZE)
        key_float = key_rows_local.astype(jnp.float32).reshape(3 * PIECE_TOKENS, KEY_VALUE_HEADS, HEAD_SIZE)
        value_float = value_rows_local.astype(jnp.float32).reshape(3 * PIECE_TOKENS, KEY_VALUE_HEADS, HEAD_SIZE)
        scores = jnp.einsum("qhgd,khd->hgqk", query_float, key_float) * query_scaling
        masked = jnp.where(allowed, scores, -jnp.inf)
        row_max = jnp.max(masked, axis=3, keepdims=True)
        exp_terms = jnp.where(allowed, jnp.exp(scores - row_max), 0.0)
        weights = exp_terms / jnp.sum(exp_terms, axis=3, keepdims=True)
        weights_bfloat = lax.optimization_barrier(weights.astype(jnp.bfloat16)).astype(jnp.float32)
        dweights = jnp.einsum("qhgd,khd->hgqk", gradient_float, value_float)
        row_dot = jnp.sum(weights * dweights, axis=3, keepdims=True)
        score_gradient = lax.optimization_barrier((weights * (dweights - row_dot)).astype(jnp.bfloat16)).astype(jnp.float32)
        grad_q = (jnp.einsum("hgqk,khd->qhgd", score_gradient, key_float) * query_scaling).reshape(PIECE_TOKENS, HQ * HEAD_SIZE).astype(jnp.bfloat16)
        key_gradient = (jnp.einsum("wyjx,jwyo->xwo", score_gradient, query_float) * query_scaling).reshape(3 * PIECE_TOKENS, KEY_VALUE_HEADS * HEAD_SIZE)
        value_gradient = jnp.einsum("wyjx,jwyo->xwo", weights_bfloat, gradient_float).reshape(3 * PIECE_TOKENS, KEY_VALUE_HEADS * HEAD_SIZE)
        return grad_q, key_gradient, value_gradient

    dq_nat, dk_terms, dv_terms = lax.map(one_piece, jnp.arange(PIECE_COUNT, dtype=jnp.int32))

    def combine(gradient_terms):
        split_rows = gradient_terms.reshape(PIECE_COUNT, 3, PIECE_TOKENS, KEY_VALUE_HEADS * HEAD_SIZE)
        empty_zero_rows = jnp.zeros((2, PIECE_TOKENS, KEY_VALUE_HEADS * HEAD_SIZE), split_rows.dtype)
        older_piece = jnp.concatenate([split_rows[2:, 0], empty_zero_rows])
        nearer_piece = jnp.concatenate([split_rows[1:, 1], empty_zero_rows[:1]])
        return (split_rows[:, 2] + nearer_piece + older_piece)[inverse_order].reshape(SEQUENCE_TOKENS, KEY_VALUE_HEADS * HEAD_SIZE).astype(jnp.bfloat16)

    grad_queries = dq_nat[inverse_order].reshape(SEQUENCE_TOKENS, HQ * HEAD_SIZE)
    return grad_queries, combine(dk_terms), combine(dv_terms)
```

```python
import math

import jax
import jax.numpy as jnp
from jax import lax
from jax.experimental import pallas as pl
from jax.experimental.pallas import tpu as pltpu
from jax.sharding import PartitionSpec as P

HEAD_SIZE = 128
WINDOW = 1024
QUERY_PER_KEY = 2
BLOCK = 128
TILE = 256
MARK = 16
NEG = -1e30

query_scaling = 168.0 ** (-0.5)
exponent_scale = query_scaling * math.log2(math.e)


def dot(a, b, ca, cb):
    return lax.dot_general(a, b, (((ca,), (cb,)), ((), ())), preferred_element_type=jnp.float32)


def pack_kernel(index_ref, starts_ref, keys_ref, values_ref, inner_ref, outer_ref):
    length = keys_ref.shape[0] // 2
    width = keys_ref.shape[1]
    blocks = length // BLOCK
    index = index_ref[0]
    parity = lax.rem(index, 2)
    for out_ref, half in ((inner_ref, 1 - parity), (outer_ref, parity)):
        rows = pl.ds(pl.multiple_of(half * length, length), length)
        out_ref[:length, :width] = keys_ref[rows, :]
        out_ref[:length, width:] = values_ref[rows, :]
        row = lax.broadcasted_iota(jnp.int32, (MARK, 2 * width), 0)
        marks = jnp.zeros((MARK, 2 * width), jnp.float32)
        for j in range(blocks):
            begin = starts_ref[half * blocks + j]
            if j == 0:
                begin = jnp.where((index == 0) & (half == 0), 1, begin)
            marks = jnp.where(row == j, begin.astype(jnp.float32), marks)
        out_ref[length:, :] = marks.astype(jnp.bfloat16)


def stage_kernel(with_half, index_ref, q_ref, g_ref, own_ref, near_ref, far_ref, *refs):
    dq_ref, own_out, near_out, far_out, acc_ref = refs[-5:]
    length = q_ref.shape[0] // 2
    width = own_ref.shape[1] // 2
    blocks = length // BLOCK
    tiles = length // TILE
    per = TILE // BLOCK
    chunks = WINDOW // TILE + 1
    index = index_ref[0]
    parity = lax.rem(index, 2)
    half = 1 - parity if with_half == "inner" else parity
    base = half * length
    pieces = (far_ref, near_ref, own_ref)

    docs = []
    count = jnp.zeros((1, TILE), jnp.float32)
    for piece in pieces:
        marks = piece[length:, :TILE].astype(jnp.float32)
        for j in range(blocks):
            count = count + marks[j : j + 1, :]
            docs.append(count)
    lane = lax.broadcasted_iota(jnp.int32, (1, TILE), 1)
    row2 = lax.broadcasted_iota(jnp.int32, (TILE, TILE), 0)
    col2 = lax.broadcasted_iota(jnp.int32, (TILE, TILE), 1)
    after = row2 > col2

    key_t = [jnp.transpose(p[:length, :width]) for p in pieces]

    started = [False] * (3 * length // TILE)
    for i in range(tiles):
        own_docs = docs[2 * blocks + i * per]
        for b in range(1, per):
            own_docs = jnp.where(lane >= b * BLOCK, docs[2 * blocks + i * per + b], own_docs)
        bias = []
        for c in range(chunks):
            bias.append(
                [jnp.where(docs[(i + c) * per + b] == own_docs, 0.0, NEG) for b in range(per)]
            )
        rows = pl.ds(pl.multiple_of(base + i * TILE, TILE), TILE)
        members = []
        for h in range(QUERY_PER_KEY):
            cols = slice(h * HEAD_SIZE, (h + 1) * HEAD_SIZE)
            qt = q_ref[rows, cols]
            gt = g_ref[rows, cols]
            scores, dweights = [], []
            top = None
            for c in range(chunks):
                p, r = divmod((i + c) * TILE, length)
                s = dot(pieces[p][r : r + TILE, :width], qt, 1, 1)
                if c == 0:
                    s = jnp.where(after, s, NEG)
                if c == chunks - 1:
                    s = jnp.where(after, NEG, s)
                scores.append(s)
                dweights.append(dot(pieces[p][r : r + TILE, width:], gt, 1, 1))
                for b in range(per):
                    t = jnp.max(s[b * BLOCK : (b + 1) * BLOCK], axis=0, keepdims=True) + bias[c][b]
                    top = t if top is None else jnp.maximum(top, t)
            shift = top * exponent_scale
            total = jnp.zeros((1, TILE), jnp.float32)
            row_dot = jnp.zeros((1, TILE), jnp.float32)
            terms = []
            for c in range(chunks):
                parts = [
                    jnp.exp2(
                        scores[c][b * BLOCK : (b + 1) * BLOCK] * exponent_scale
                        + (bias[c][b] - shift)
                    )
                    for b in range(per)
                ]
                e = jnp.concatenate(parts, axis=0)
                terms.append(e)
                total = total + jnp.sum(e, axis=0, keepdims=True)
                row_dot = row_dot + jnp.sum(e * dweights[c], axis=0, keepdims=True)
            inverse = 1.0 / total
            row_dot = row_dot * inverse
            weights, dscores = [], []
            dq_t = jnp.zeros((width, TILE), jnp.float32)
            for c in range(chunks):
                w = terms[c] * inverse
                ds = (w * (dweights[c] - row_dot)).astype(jnp.bfloat16)
                weights.append(w.astype(jnp.bfloat16))
                dscores.append(ds)
                p, r = divmod((i + c) * TILE, length)
                dq_t = dq_t + dot(key_t[p][:, r : r + TILE], ds, 1, 0)
            dq_ref[rows, cols] = jnp.transpose(dq_t * query_scaling).astype(jnp.bfloat16)
            members.append((qt, gt, weights, dscores))
        q_all = jnp.concatenate([m[0] for m in members], axis=0)
        g_all = jnp.concatenate([m[1] for m in members], axis=0)
        for c in range(chunks):
            w_all = jnp.concatenate([m[2][c] for m in members], axis=1)
            d_all = jnp.concatenate([m[3][c] for m in members], axis=1)
            dk = dot(d_all, q_all, 1, 0) * query_scaling
            dv = dot(w_all, g_all, 1, 0)
            slot = i + c
            at = slice(slot * TILE, (slot + 1) * TILE)
            if started[slot]:
                dk = dk + acc_ref[at, :width]
                dv = dv + acc_ref[at, width:]
            started[slot] = True
            acc_ref[at, :width] = dk
            acc_ref[at, width:] = dv
    if len(refs) == 6:
        other = pl.ds(pl.multiple_of(length - base, length), length)
        dq_ref[other, :] = refs[0][other, :]
    far_out[...] = acc_ref[:length].astype(jnp.bfloat16)
    near_out[...] = acc_ref[length : 2 * length].astype(jnp.bfloat16)
    own_out[...] = acc_ref[2 * length :]


def sum_kernel(index_ref, inner_own, inner_a, inner_b, outer_own, outer_a, outer_b, dk_ref, dv_ref):
    length = inner_own.shape[0]
    width = dk_ref.shape[1]
    parity = lax.rem(index_ref[0], 2)
    f32 = jnp.float32
    for half, own, a, b in (
        (1 - parity, inner_own, inner_a, inner_b),
        (parity, outer_own, outer_a, outer_b),
    ):
        rows = pl.ds(pl.multiple_of(half * length, length), length)
        total = own[...] + (a[...].astype(f32) + b[...].astype(f32))
        dk_ref[rows, :] = total[:, :width].astype(jnp.bfloat16)
        dv_ref[rows, :] = total[:, width:].astype(jnp.bfloat16)


def smem():
    return pl.BlockSpec(memory_space=pltpu.SMEM)


def vmem():
    return pl.BlockSpec(memory_space=pltpu.VMEM)


LIMIT = pltpu.CompilerParams(vmem_limit_bytes=48 * 1024 * 1024)


def on_device(queries, keys, values, grad_out, starts):
    length = keys.shape[0] // 2
    width = keys.shape[1]
    count = lax.axis_size("seq")
    index = lax.axis_index("seq").astype(jnp.int32).reshape(1)
    order = list(range(0, count, 2)) + list(range(count - 1, 0, -2))
    clockwise = [(order[k], order[(k + 1) % count]) for k in range(count)]
    counter = [(b, a) for a, b in clockwise]
    pairs = [(d, d ^ 1) for d in range(count)]
    follow = dict(clockwise)
    across = [(d, follow[d ^ 1]) for d in range(count)]

    packed = jax.ShapeDtypeStruct((length + MARK, 2 * width), jnp.bfloat16)
    inner, outer = pl.pallas_call(
        pack_kernel,
        out_shape=(packed, packed),
        in_specs=[smem(), smem(), vmem(), vmem()],
        out_specs=(vmem(), vmem()),
    )(index, starts, keys, values)

    inner_far = lax.ppermute(inner, "seq", counter)
    outer_far = lax.ppermute(outer, "seq", clockwise)
    inner_near = lax.ppermute(outer, "seq", pairs)
    outer_near = lax.ppermute(inner_far, "seq", pairs)

    def stage(which, own, near, far, dq):
        wide = jax.ShapeDtypeStruct((length, 2 * width), jnp.float32)
        narrow = jax.ShapeDtypeStruct((length, 2 * width), jnp.bfloat16)
        operands = [index, queries, grad_out, own, near, far]
        specs = [smem()] + [vmem()] * 5
        aliases = {}
        if dq is not None:
            aliases = {len(operands): 0}
            operands.append(dq)
            specs.append(pl.BlockSpec(memory_space=pltpu.VMEM))
        flops = 10 * QUERY_PER_KEY * length * (WINDOW + TILE) * width
        return pl.pallas_call(
            lambda *refs: stage_kernel(which, *refs),
            out_shape=(jax.ShapeDtypeStruct(queries.shape, jnp.bfloat16), wide, narrow, narrow),
            in_specs=specs,
            out_specs=(vmem(),) * 4,
            scratch_shapes=[pltpu.VMEM((3 * length, 2 * width), jnp.float32)],
            input_output_aliases=aliases,
            compiler_params=LIMIT,
            cost_estimate=pl.CostEstimate(
                flops=flops, bytes_accessed=4 * 1024 * 1024, transcendentals=0
            ),
            name=which + "_stage",
        )(*operands)

    dq, inner_own, inner_g1, inner_g2 = stage("inner", inner, inner_near, inner_far, None)
    outer_b = lax.ppermute(inner_g1, "seq", pairs)
    inner_b = lax.ppermute(inner_g2, "seq", clockwise)
    dq, outer_own, outer_g1, outer_g2 = stage("outer", outer, outer_near, outer_far, dq)
    inner_a = lax.ppermute(outer_g1, "seq", across)
    outer_a = lax.ppermute(outer_g2, "seq", counter)

    half = jax.ShapeDtypeStruct(keys.shape, jnp.bfloat16)
    dk, dv = pl.pallas_call(
        sum_kernel,
        out_shape=(half, half),
        in_specs=[smem()] + [vmem()] * 6,
        out_specs=(vmem(), vmem()),
    )(index, inner_own, inner_a, inner_b, outer_own, outer_a, outer_b)
    return dq, dk, dv


def solution(mesh):
    in_specs = (P("seq", "head"), P("seq", "head"), P("seq", "head"), P("seq", "head"), P("seq"))
    out_specs = (P("seq", "head"), P("seq", "head"), P("seq", "head"))
    return jax.shard_map(
        on_device, mesh=mesh, in_specs=in_specs, out_specs=out_specs, check_vma=False
    )
```

```python
import math

import jax
import jax.numpy as jnp
from jax import lax
from jax.experimental import pallas as pl
from jax.experimental.pallas import tpu as pltpu
from jax.sharding import PartitionSpec as P

HEAD_SIZE = 128
WINDOW = 1024
QUERY_PER_KEY = 2
BLOCK = 128
TILE = 256
MARK = 16
NEG = -1e30

query_scaling = 168.0 ** (-0.5)
exponent_scale = query_scaling * math.log2(math.e)


def dot(a, b, ca, cb):
    return lax.dot_general(a, b, (((ca,), (cb,)), ((), ())), preferred_element_type=jnp.float32)


def halves(index):
    parity = lax.rem(index, 2)
    even = lax.rem(parity + lax.div(index, 2), 2) == 0
    return 1 - parity, parity, even


def pack_half(keys, values, starts, half, place):
    length = keys.shape[0] // 2
    width = keys.shape[1]
    blocks = length // BLOCK
    both = [lax.dynamic_slice_in_dim(x, half * length, length, 0) for x in (keys, values)]
    begins = lax.dynamic_slice_in_dim(starts, half * blocks, blocks, 0)
    first = (lax.iota(jnp.int32, blocks) == 0) & (place == 0) & (half == 0)
    begins = jnp.pad(jnp.where(first, 1, begins).astype(jnp.bfloat16), (0, MARK - blocks))
    marks = jnp.broadcast_to(begins[:, None], (MARK, 2 * width))
    return jnp.concatenate([jnp.concatenate(both, axis=1), marks], axis=0)


def stage_kernel(with_half, index_ref, q_ref, g_ref, own_ref, near_ref, far_ref, *refs):
    dq_ref, own_out, near_out, far_out, acc_ref = refs[-5:]
    length = q_ref.shape[0] // 2
    width = own_ref.shape[1] // 2
    blocks = length // BLOCK
    tiles = length // TILE
    per = TILE // BLOCK
    chunks = WINDOW // TILE + 1
    index = index_ref[0]
    parity = lax.rem(index, 2)
    half = 1 - parity if with_half == "inner" else parity
    base = half * length
    pieces = (far_ref, near_ref, own_ref)

    docs = []
    count = jnp.zeros((1, TILE), jnp.float32)
    for piece in pieces:
        marks = piece[length:, :TILE].astype(jnp.float32)
        for j in range(blocks):
            count = count + marks[j : j + 1, :]
            docs.append(count)
    lane = lax.broadcasted_iota(jnp.int32, (1, TILE), 1)
    row2 = lax.broadcasted_iota(jnp.int32, (TILE, TILE), 0)
    col2 = lax.broadcasted_iota(jnp.int32, (TILE, TILE), 1)
    after = row2 > col2

    key_t = [jnp.transpose(p[:length, :width]) for p in pieces]

    started = [False] * (3 * length // TILE)
    for i in range(tiles):
        own_docs = docs[2 * blocks + i * per]
        for b in range(1, per):
            own_docs = jnp.where(lane >= b * BLOCK, docs[2 * blocks + i * per + b], own_docs)
        bias = []
        for c in range(chunks):
            bias.append(
                [jnp.where(docs[(i + c) * per + b] == own_docs, 0.0, NEG) for b in range(per)]
            )
        rows = pl.ds(pl.multiple_of(base + i * TILE, TILE), TILE)
        members = []
        for h in range(QUERY_PER_KEY):
            cols = slice(h * HEAD_SIZE, (h + 1) * HEAD_SIZE)
            qt = q_ref[rows, cols]
            gt = g_ref[rows, cols]
            scores, dweights = [], []
            top = None
            for c in range(chunks):
                p, r = divmod((i + c) * TILE, length)
                s = dot(pieces[p][r : r + TILE, :width], qt, 1, 1)
                if c == 0:
                    s = jnp.where(after, s, NEG)
                if c == chunks - 1:
                    s = jnp.where(after, NEG, s)
                scores.append(s)
                dweights.append(dot(pieces[p][r : r + TILE, width:], gt, 1, 1))
                for b in range(per):
                    t = jnp.max(s[b * BLOCK : (b + 1) * BLOCK], axis=0, keepdims=True) + bias[c][b]
                    top = t if top is None else jnp.maximum(top, t)
            shift = top * exponent_scale
            total = jnp.zeros((1, TILE), jnp.float32)
            row_dot = jnp.zeros((1, TILE), jnp.float32)
            terms = []
            for c in range(chunks):
                parts = [
                    jnp.exp2(
                        scores[c][b * BLOCK : (b + 1) * BLOCK] * exponent_scale
                        + (bias[c][b] - shift)
                    )
                    for b in range(per)
                ]
                e = jnp.concatenate(parts, axis=0)
                terms.append(e)
                total = total + jnp.sum(e, axis=0, keepdims=True)
                row_dot = row_dot + jnp.sum(e * dweights[c], axis=0, keepdims=True)
            inverse = 1.0 / total
            row_dot = row_dot * inverse
            weights, dscores = [], []
            dq_t = jnp.zeros((width, TILE), jnp.float32)
            for c in range(chunks):
                w = terms[c] * inverse
                ds = (w * (dweights[c] - row_dot)).astype(jnp.bfloat16)
                weights.append(w.astype(jnp.bfloat16))
                dscores.append(ds)
                p, r = divmod((i + c) * TILE, length)
                dq_t = dq_t + dot(key_t[p][:, r : r + TILE], ds, 1, 0)
            dq_ref[rows, cols] = jnp.transpose(dq_t * query_scaling).astype(jnp.bfloat16)
            members.append((qt, gt, weights, dscores))
        q_all = jnp.concatenate([m[0] for m in members], axis=0)
        g_all = jnp.concatenate([m[1] for m in members], axis=0)
        for c in range(chunks):
            w_all = jnp.concatenate([m[2][c] for m in members], axis=1)
            d_all = jnp.concatenate([m[3][c] for m in members], axis=1)
            dk = dot(d_all, q_all, 1, 0) * query_scaling
            dv = dot(w_all, g_all, 1, 0)
            slot = i + c
            at = slice(slot * TILE, (slot + 1) * TILE)
            if started[slot]:
                dk = dk + acc_ref[at, :width]
                dv = dv + acc_ref[at, width:]
            started[slot] = True
            acc_ref[at, :width] = dk
            acc_ref[at, width:] = dv
    if len(refs) == 6:
        other = pl.ds(pl.multiple_of(length - base, length), length)
        dq_ref[other, :] = refs[0][other, :]
    far_out[...] = acc_ref[:length].astype(jnp.bfloat16)
    near_out[...] = acc_ref[length : 2 * length].astype(jnp.bfloat16)
    own_out[...] = acc_ref[2 * length :]


def block_docs(pieces, length):
    docs = []
    count = jnp.zeros((1, TILE), jnp.float32)
    for piece in pieces:
        marks = piece[length:, :TILE].astype(jnp.float32)
        for j in range(length // BLOCK):
            count = count + marks[j : j + 1, :]
            docs.append(count)
    return docs


def tile_docs(docs, first):
    lane = lax.broadcasted_iota(jnp.int32, (1, TILE), 1)
    own = docs[first]
    for b in range(1, TILE // BLOCK):
        own = jnp.where(lane >= b * BLOCK, docs[first + b], own)
    return own


def chunk_list(tile, length, wanted):
    found = []
    for c in range(WINDOW // TILE + 1):
        piece, row = divmod((tile + c) * TILE, length)
        if piece in wanted:
            found.append((c, piece, row))
    return found


def triangle():
    row = lax.broadcasted_iota(jnp.int32, (TILE, TILE), 0)
    return row > lax.broadcasted_iota(jnp.int32, (TILE, TILE), 1)


def masked_scores(c, keys, qt, after):
    s = dot(keys, qt, 1, 1)
    if c == 0:
        s = jnp.where(after, s, NEG)
    if c == WINDOW // TILE:
        s = jnp.where(after, NEG, s)
    return s


def bias_rows(docs, first, own):
    return [jnp.where(docs[first + b] == own, 0.0, NEG) for b in range(TILE // BLOCK)]


def chunk_top(s, bias, top):
    for b, row in enumerate(bias):
        t = jnp.max(s[b * BLOCK : (b + 1) * BLOCK], axis=0, keepdims=True) + row
        top = t if top is None else jnp.maximum(top, t)
    return top


def chunk_terms(s, bias, shift):
    return jnp.concatenate(
        [
            jnp.exp2(s[b * BLOCK : (b + 1) * BLOCK] * exponent_scale + (row - shift))
            for b, row in enumerate(bias)
        ],
        axis=0,
    )


def softmax_part(parts):
    top = None
    for s, dw, bias in parts:
        top = chunk_top(s, bias, top)
    shift = top * exponent_scale
    total = jnp.zeros((1, TILE), jnp.float32)
    mixed = jnp.zeros((1, TILE), jnp.float32)
    for s, dw, bias in parts:
        e = chunk_terms(s, bias, shift)
        total = total + jnp.sum(e, axis=0, keepdims=True)
        mixed = mixed + jnp.sum(e * dw, axis=0, keepdims=True)
    return top, total, mixed


def outer_stats_kernel(index_ref, q_ref, g_ref, own_ref, far_ref, stats_ref):
    length = q_ref.shape[0] // 2
    width = own_ref.shape[1] // 2
    blocks = length // BLOCK
    base = lax.rem(index_ref[0], 2) * length
    docs = block_docs((far_ref, own_ref), length)
    after = triangle()
    for i in range(length // TILE):
        own_docs = tile_docs(docs, blocks + i * (TILE // BLOCK))
        rows = pl.ds(pl.multiple_of(base + i * TILE, TILE), TILE)
        for h in range(QUERY_PER_KEY):
            cols = slice(h * HEAD_SIZE, (h + 1) * HEAD_SIZE)
            qt, gt = q_ref[rows, cols], g_ref[rows, cols]
            for n, (piece, ref, first) in enumerate(((2, own_ref, blocks), (0, far_ref, 0))):
                parts = []
                for c, _, r in chunk_list(i, length, (piece,)):
                    s = masked_scores(c, ref[r : r + TILE, :width], qt, after)
                    dw = dot(ref[r : r + TILE, width:], gt, 1, 1)
                    parts.append((s, dw, bias_rows(docs, first + r // BLOCK, own_docs)))
                for k, value in enumerate(softmax_part(parts)):
                    at = (h * 2 + n) * 3 + k
                    stats_ref[at : at + 1, i * TILE : (i + 1) * TILE] = value


def outer_near_kernel(
    index_ref, q_ref, g_ref, own_ref, near_ref, part_ref, near_out, dq_out, stats_ref, acc_ref
):
    length = q_ref.shape[0] // 2
    width = own_ref.shape[1] // 2
    blocks = length // BLOCK
    base = lax.rem(index_ref[0], 2) * length
    docs = block_docs((near_ref, own_ref), length)
    far_bias = jnp.where(docs[blocks - 1] == 0.0, 0.0, NEG)
    key_t = jnp.transpose(near_ref[:length, :width])
    for i in range(length // TILE):
        own_docs = tile_docs(docs, blocks + i * (TILE // BLOCK))
        rows = pl.ds(pl.multiple_of(base + i * TILE, TILE), TILE)
        lanes = slice(i * TILE, (i + 1) * TILE)
        members = []
        chunks = chunk_list(i, length, (1,))
        for h in range(QUERY_PER_KEY):
            cols = slice(h * HEAD_SIZE, (h + 1) * HEAD_SIZE)
            qt, gt = q_ref[rows, cols], g_ref[rows, cols]
            at = h * 6
            own_top, own_total, own_mixed = [part_ref[at + k : at + k + 1, lanes] for k in range(3)]
            far_top, far_total, far_mixed = [
                part_ref[at + 3 + k : at + 4 + k, lanes] for k in range(3)
            ]
            top = jnp.maximum(own_top, far_top + far_bias)
            parts = []
            for c, _, r in chunks:
                s = dot(near_ref[r : r + TILE, :width], qt, 1, 1)
                dw = dot(near_ref[r : r + TILE, width:], gt, 1, 1)
                bias = bias_rows(docs, r // BLOCK, own_docs)
                top = chunk_top(s, bias, top)
                parts.append((s, dw, bias))
            shift = top * exponent_scale
            own_scale = jnp.exp2(own_top * exponent_scale - shift)
            far_scale = jnp.exp2(far_top * exponent_scale + (far_bias - shift))
            total = own_total * own_scale + far_total * far_scale
            mixed = own_mixed * own_scale + far_mixed * far_scale
            terms = []
            for s, dw, bias in parts:
                e = chunk_terms(s, bias, shift)
                terms.append(e)
                total = total + jnp.sum(e, axis=0, keepdims=True)
                mixed = mixed + jnp.sum(e * dw, axis=0, keepdims=True)
            inverse = 1.0 / total
            row_dot = mixed * inverse
            for k, value in enumerate((shift, inverse, row_dot)):
                stats_ref[h * 3 + k : h * 3 + k + 1, lanes] = value
            weights, dscores = [], []
            dq_t = jnp.zeros((width, TILE), jnp.float32)
            for e, (s, dw, bias), (c, _, r) in zip(terms, parts, chunks):
                w = e * inverse
                ds = (w * (dw - row_dot)).astype(jnp.bfloat16)
                weights.append(w.astype(jnp.bfloat16))
                dscores.append(ds)
                dq_t = dq_t + dot(key_t[:, r : r + TILE], ds, 1, 0)
            dq_out[h * width : (h + 1) * width, lanes] = dq_t
            members.append((qt, gt, weights, dscores))
        add_key_grads(acc_ref, members, [r for _, _, r in chunks], i == 0)
    near_out[...] = acc_ref[...].astype(jnp.bfloat16)


def add_key_grads(acc_ref, members, slots, first):
    width = acc_ref.shape[1] // 2
    q_all = jnp.concatenate([m[0] for m in members], axis=0)
    g_all = jnp.concatenate([m[1] for m in members], axis=0)
    for n, slot in enumerate(slots):
        w_all = jnp.concatenate([m[2][n] for m in members], axis=1)
        d_all = jnp.concatenate([m[3][n] for m in members], axis=1)
        dk = dot(d_all, q_all, 1, 0) * query_scaling
        dv = dot(w_all, g_all, 1, 0)
        at = slice(slot, slot + TILE)
        fresh = first if isinstance(first, bool) else slot in first
        if not fresh:
            dk = dk + acc_ref[at, :width]
            dv = dv + acc_ref[at, width:]
        acc_ref[at, :width] = dk
        acc_ref[at, width:] = dv


def outer_share_kernel(
    wanted, last, index_ref, q_ref, g_ref, own_ref, near_ref, far_ref, stats_ref, dq_part_ref, *refs
):
    length = q_ref.shape[0] // 2
    width = own_ref.shape[1] // 2
    blocks = length // BLOCK
    base = lax.rem(index_ref[0], 2) * length
    if wanted == 2:
        dq_in, dq_ref, grad_out, acc_ref = refs
    else:
        inner_near_ref, inner_far_ref, dq_ref, pair_out, first_out, second_out, acc_ref = refs
    docs = block_docs((far_ref, near_ref, own_ref), length)
    after = triangle()
    piece = own_ref if wanted == 2 else far_ref
    key_t = jnp.transpose(piece[:length, :width])
    seen = set()
    for i in range(length // TILE):
        own_docs = tile_docs(docs, 2 * blocks + i * (TILE // BLOCK))
        rows = pl.ds(pl.multiple_of(base + i * TILE, TILE), TILE)
        lanes = slice(i * TILE, (i + 1) * TILE)
        members = []
        chunks = chunk_list(i, length, (wanted,))
        for h in range(QUERY_PER_KEY):
            cols = slice(h * HEAD_SIZE, (h + 1) * HEAD_SIZE)
            qt, gt = q_ref[rows, cols], g_ref[rows, cols]
            shift, inverse, row_dot = [
                stats_ref[h * 3 + k : h * 3 + k + 1, lanes] for k in range(3)
            ]
            weights, dscores = [], []
            dq_t = dq_part_ref[h * width : (h + 1) * width, lanes]
            for c, p, r in chunks:
                s = masked_scores(c, piece[r : r + TILE, :width], qt, after)
                dw = dot(piece[r : r + TILE, width:], gt, 1, 1)
                bias = bias_rows(docs, p * blocks + r // BLOCK, own_docs)
                w = chunk_terms(s, bias, shift) * inverse
                ds = (w * (dw - row_dot)).astype(jnp.bfloat16)
                weights.append(w.astype(jnp.bfloat16))
                dscores.append(ds)
                dq_t = dq_t + dot(key_t[:, r : r + TILE], ds, 1, 0)
            if wanted == 2:
                dq_ref[rows, cols] = jnp.transpose(dq_t * query_scaling).astype(jnp.bfloat16)
            else:
                dq_ref[h * width : (h + 1) * width, lanes] = dq_t
            members.append((qt, gt, weights, dscores))
        slots = [r for _, _, r in chunks]
        add_key_grads(acc_ref, members, slots, [x for x in slots if x not in seen])
        seen.update(slots)
    if wanted == 2:
        other = pl.ds(pl.multiple_of(length - base, length), length)
        dq_ref[other, :] = dq_in[other, :]
        grad_out[...] = acc_ref[...]
    else:
        index = index_ref[0]
        _, _, even = halves(index)
        grad = acc_ref[...]
        pair = inner_near_ref[...].astype(jnp.float32) + jnp.where(index == last, grad, 0.0)
        pair_out[...] = pair.astype(jnp.bfloat16)
        grad = grad.astype(jnp.bfloat16)
        other = inner_far_ref[...]
        first_out[...] = jnp.where(even, other, grad)
        second_out[...] = jnp.where(even, grad, other)


def early_sum_kernel(own, across, out):
    out[...] = own[...] + across[...].astype(jnp.float32)


def sum_kernel(index_ref, inner_own, outer_own, pair, first, second, dk_ref, dv_ref):
    length = inner_own.shape[0]
    width = dk_ref.shape[1]
    inner, outer, even = halves(index_ref[0])
    f32 = jnp.float32
    one, two = first[...].astype(f32), second[...].astype(f32)
    for half, total in (
        (inner, inner_own[...] + jnp.where(even, two, one)),
        (outer, outer_own[...] + (pair[...].astype(f32) + jnp.where(even, one, two))),
    ):
        rows = pl.ds(pl.multiple_of(half * length, length), length)
        dk_ref[rows, :] = total[:, :width].astype(jnp.bfloat16)
        dv_ref[rows, :] = total[:, width:].astype(jnp.bfloat16)


def smem():
    return pl.BlockSpec(memory_space=pltpu.SMEM)


def hbm():
    return pl.BlockSpec(memory_space=pltpu.HBM)


def vmem():
    return pl.BlockSpec(memory_space=pltpu.VMEM)


LIMIT = pltpu.CompilerParams(vmem_limit_bytes=16 * 1024 * 1024)
SMALL = pltpu.CompilerParams(vmem_limit_bytes=4 * 1024 * 1024)


def on_device(queries, keys, values, grad_out, starts):
    length = keys.shape[0] // 2
    width = keys.shape[1]
    count = lax.axis_size("seq")
    index = lax.axis_index("seq").astype(jnp.int32).reshape(1)
    assert count % 4 == 0
    last = count - 1
    pairs = [(d, d ^ 1) for d in range(count)]
    first = [(d, d ^ 2) for d in range(count)]
    second = [(d, ((d - 2) ^ 2) + 2) for d in range(2, count - 2)]
    across = [(d, d + 1 if d % 2 else d - 1) for d in range(1, last)] + [(last, last)]
    _, _, even = halves(index[0])

    bf16, f32 = jnp.bfloat16, jnp.float32
    narrow = jax.ShapeDtypeStruct((length, 2 * width), bf16)
    wide = jax.ShapeDtypeStruct((length, 2 * width), f32)
    rows = jax.ShapeDtypeStruct((16, length), f32)
    like_q = jax.ShapeDtypeStruct(queries.shape, bf16)
    unit = 2 * QUERY_PER_KEY * TILE * TILE * width

    def call(kernel, outs, operands, name, work, scratch=(), specs=None, limit=LIMIT, alias=None,
             out_specs=None):
        return pl.pallas_call(
            kernel,
            out_shape=outs,
            in_specs=specs or [smem()] + [vmem()] * (len(operands) - 1),
            out_specs=out_specs or (vmem(),) * len(outs),
            scratch_shapes=list(scratch),
            input_output_aliases=alias or {},
            compiler_params=limit,
            cost_estimate=pl.CostEstimate(
                flops=unit * work, bytes_accessed=1024 * 1024, transcendentals=0
            ),
            name=name,
        )(*operands)

    place = index[0]
    parity = lax.rem(place, 2)
    inner = pack_half(keys, values, starts, 1 - parity, place)
    outer = pack_half(keys, values, starts, parity, place)
    give_1 = jnp.where(even, outer, inner)
    give_2 = jnp.where(even, inner, outer)

    take_1 = lax.ppermute(give_1, "seq", first)
    take_2 = lax.ppermute(give_2, "seq", second + [(last - 1, last), (last, last - 1), (0, 1), (1, 0)])
    inner_near = lax.ppermute(outer, "seq", pairs)
    inner_far = jnp.where(even, take_1, take_2)
    outer_far = jnp.where(even, take_2, take_1)
    q, g = queries, grad_out
    outer_near = lax.ppermute(inner_far, "seq", pairs)

    def after(value, *others):
        return lax.optimization_barrier((value,) + others)[0]

    grads = pltpu.VMEM((length, 2 * width), f32)
    dq_rows = jax.ShapeDtypeStruct((QUERY_PER_KEY * width, length), f32)

    (part,) = call(
        outer_stats_kernel, (rows,), (index, q, g, outer, outer_far), "outer_stats", 12
    )
    dq, inner_own, inner_g1, inner_g2 = call(
        lambda *refs: stage_kernel("inner", *refs),
        (like_q, wide, narrow, narrow),
        (index, after(q, part), g, inner, inner_near, inner_far),
        "inner_stage",
        50,
        [pltpu.VMEM((3 * length, 2 * width), f32)],
    )
    outer_g1, dq_part, stats = call(
        outer_near_kernel,
        (narrow, dq_rows, rows),
        (index, after(q, dq), g, outer, outer_near, part),
        "outer_near",
        20,
        [grads],
    )
    inner_a = lax.ppermute(outer_g1, "seq", across)
    dq_part, pair_give, give_1, give_2 = call(
        lambda *refs: outer_share_kernel(0, last, *refs),
        (dq_rows, narrow, narrow, narrow),
        (index, q, g, outer, outer_near, outer_far, stats, dq_part, inner_g1, inner_g2),
        "outer_far",
        15,
        [grads],
    )
    pair_take = lax.ppermute(pair_give, "seq", pairs)
    take_1 = lax.ppermute(give_1, "seq", first)
    take_2 = lax.ppermute(give_2, "seq", second + [(last - 1, last)])
    dq, outer_own = call(
        lambda *refs: outer_share_kernel(2, last, *refs),
        (like_q, wide),
        (index, q, g, outer, outer_near, outer_far, stats, dq_part, dq),
        "outer_own",
        15,
        [grads],
        alias={8: 0},
    )
    (inner_own,) = call(
        early_sum_kernel,
        (wide,),
        (inner_own, inner_a),
        "early_sum",
        0,
        specs=[vmem(), vmem()],
        limit=SMALL,
    )
    half = jax.ShapeDtypeStruct(keys.shape, bf16)
    dk, dv = call(
        sum_kernel,
        (half, half),
        (index, inner_own, outer_own, pair_take, take_1, take_2),
        "sum",
        1,
        limit=SMALL,
    )
    return dq, dk, dv


def solution(mesh):
    in_specs = (P("seq", "head"), P("seq", "head"), P("seq", "head"), P("seq", "head"), P("seq"))
    out_specs = (P("seq", "head"), P("seq", "head"), P("seq", "head"))
    return jax.shard_map(
        on_device, mesh=mesh, in_specs=in_specs, out_specs=out_specs, check_vma=False
    )
```

```python
import math

import jax
import jax.numpy as jnp
from jax import lax
from jax.experimental import pallas as pl
from jax.experimental.pallas import tpu as pltpu
from jax.sharding import PartitionSpec as P

HEAD_SIZE = 128
WINDOW = 1024
QUERY_PER_KEY = 2
BLOCK = 128
TILE = 256
MARK = 16
NEG = -1e30

query_scaling = 168.0 ** (-0.5)
exponent_scale = query_scaling * math.log2(math.e)


def dot(a, b, ca, cb):
    return lax.dot_general(a, b, (((ca,), (cb,)), ((), ())), preferred_element_type=jnp.float32)


def halves(index):
    parity = lax.rem(index, 2)
    even = lax.rem(parity + lax.div(index, 2), 2) == 0
    return 1 - parity, parity, even


def pack_half(keys, values, starts, half, place):
    length = keys.shape[0] // 2
    width = keys.shape[1]
    blocks = length // BLOCK
    both = [lax.dynamic_slice_in_dim(x, half * length, length, 0) for x in (keys, values)]
    starts = lax.optimization_barrier((starts, *both))[0]
    begins = lax.dynamic_slice_in_dim(starts, half * blocks, blocks, 0)
    first = (lax.iota(jnp.int32, blocks) == 0) & (place == 0) & (half == 0)
    begins = jnp.pad(jnp.where(first, 1, begins).astype(jnp.bfloat16), (0, MARK - blocks))
    marks = jnp.broadcast_to(begins[:, None], (MARK, 2 * width))
    return jnp.concatenate([jnp.concatenate(both, axis=1), marks], axis=0)


def inner_stage_kernel(
    index_ref, q_ref, g_ref, own_ref, near_ref, far_ref,
    dq_ref, own_out, near_out, far_out, acc_ref,
):
    length = q_ref.shape[0] // 2
    width = own_ref.shape[1] // 2
    blocks = length // BLOCK
    base = (1 - lax.rem(index_ref[0], 2)) * length
    pieces = (far_ref, near_ref, own_ref)
    docs = block_docs(pieces, length)
    after = triangle()
    key_t = [jnp.transpose(p[:length, :width]) for p in pieces]
    steps = [(i, h) for i in range(length // TILE) for h in range(QUERY_PER_KEY)]

    def products(i, h):
        rows = pl.ds(pl.multiple_of(base + i * TILE, TILE), TILE)
        cols = slice(h * HEAD_SIZE, (h + 1) * HEAD_SIZE)
        qt, gt = q_ref[rows, cols], g_ref[rows, cols]
        own_docs = tile_docs(docs, 2 * blocks + i * (TILE // BLOCK))
        parts = []
        for c, p, r in chunk_list(i, length, (0, 1, 2)):
            s = masked_scores(c, pieces[p][r : r + TILE, :width], qt, after)
            dw = dot(pieces[p][r : r + TILE, width:], gt, 1, 1)
            parts.append((s, dw, bias_rows(docs, p * blocks + r // BLOCK, own_docs)))
        return qt, gt, parts

    def shares(i, h, parts):
        top = None
        for s, dw, bias in parts:
            top = chunk_top(s, bias, top)
        shift = top * exponent_scale
        total = jnp.zeros((1, TILE), jnp.float32)
        mixed = jnp.zeros((1, TILE), jnp.float32)
        terms = []
        for s, dw, bias in parts:
            e = chunk_terms(s, bias, shift)
            terms.append(e)
            total = total + jnp.sum(e, axis=0, keepdims=True)
            mixed = mixed + jnp.sum(e * dw, axis=0, keepdims=True)
        inverse = 1.0 / total
        row_dot = mixed * inverse
        weights, dscores = [], []
        for e, (s, dw, bias) in zip(terms, parts):
            w = e * inverse
            dscores.append((w * (dw - row_dot)).astype(jnp.bfloat16))
            weights.append(w.astype(jnp.bfloat16))
        return weights, dscores

    def query_grad(i, h, dscores):
        dq_t = jnp.zeros((width, TILE), jnp.float32)
        for ds, (c, p, r) in zip(dscores, chunk_list(i, length, (0, 1, 2))):
            dq_t = dq_t + dot(key_t[p][:, r : r + TILE], ds, 1, 0)
        dq_ref[h * width : (h + 1) * width, i * TILE : (i + 1) * TILE] = dq_t

    seen = set()
    members = []
    ready = products(*steps[0])
    for n, (i, h) in enumerate(steps):
        qt, gt, parts = ready
        if n + 1 < len(steps):
            ready = products(*steps[n + 1])
        weights, dscores = shares(i, h, parts)
        query_grad(i, h, dscores)
        members.append((qt, gt, weights, dscores))
        if h == QUERY_PER_KEY - 1:
            slots = [p * length + r for _, p, r in chunk_list(i, length, (0, 1, 2))]
            add_key_grads(acc_ref, members, slots, [x for x in slots if x not in seen])
            seen.update(slots)
            members = []
    far_out[...] = acc_ref[:length].astype(jnp.bfloat16)
    near_out[...] = acc_ref[length : 2 * length].astype(jnp.bfloat16)
    own_out[...] = acc_ref[2 * length :]


def block_docs(pieces, length):
    docs = []
    count = jnp.zeros((1, TILE), jnp.float32)
    for piece in pieces:
        marks = piece[length:, :TILE].astype(jnp.float32)
        for j in range(length // BLOCK):
            count = count + marks[j : j + 1, :]
            docs.append(count)
    return docs


def tile_docs(docs, first):
    lane = lax.broadcasted_iota(jnp.int32, (1, TILE), 1)
    own = docs[first]
    for b in range(1, TILE // BLOCK):
        own = jnp.where(lane >= b * BLOCK, docs[first + b], own)
    return own


def chunk_list(tile, length, wanted):
    found = []
    for c in range(WINDOW // TILE + 1):
        piece, row = divmod((tile + c) * TILE, length)
        if piece in wanted:
            found.append((c, piece, row))
    return found


def triangle():
    row = lax.broadcasted_iota(jnp.int32, (TILE, TILE), 0)
    return row > lax.broadcasted_iota(jnp.int32, (TILE, TILE), 1)


def masked_scores(c, keys, qt, after):
    s = dot(keys, qt, 1, 1)
    if c == 0:
        s = jnp.where(after, s, NEG)
    if c == WINDOW // TILE:
        s = jnp.where(after, NEG, s)
    return s


def bias_rows(docs, first, own):
    return [jnp.where(docs[first + b] == own, 0.0, NEG) for b in range(TILE // BLOCK)]


def chunk_top(s, bias, top):
    for b, row in enumerate(bias):
        t = jnp.max(s[b * BLOCK : (b + 1) * BLOCK], axis=0, keepdims=True) + row
        top = t if top is None else jnp.maximum(top, t)
    return top


def chunk_terms(s, bias, shift):
    return jnp.concatenate(
        [
            jnp.exp2(s[b * BLOCK : (b + 1) * BLOCK] * exponent_scale + (row - shift))
            for b, row in enumerate(bias)
        ],
        axis=0,
    )


def softmax_part(parts):
    top = None
    for s, dw, bias in parts:
        top = chunk_top(s, bias, top)
    shift = top * exponent_scale
    total = jnp.zeros((1, TILE), jnp.float32)
    mixed = jnp.zeros((1, TILE), jnp.float32)
    for s, dw, bias in parts:
        e = chunk_terms(s, bias, shift)
        total = total + jnp.sum(e, axis=0, keepdims=True)
        mixed = mixed + jnp.sum(e * dw, axis=0, keepdims=True)
    return top, total, mixed


def outer_stats_kernel(index_ref, q_ref, g_ref, own_ref, far_ref, stats_ref):
    length = q_ref.shape[0] // 2
    width = own_ref.shape[1] // 2
    blocks = length // BLOCK
    base = lax.rem(index_ref[0], 2) * length
    docs = block_docs((far_ref, own_ref), length)
    after = triangle()
    for i in range(length // TILE):
        own_docs = tile_docs(docs, blocks + i * (TILE // BLOCK))
        rows = pl.ds(pl.multiple_of(base + i * TILE, TILE), TILE)
        for h in range(QUERY_PER_KEY):
            cols = slice(h * HEAD_SIZE, (h + 1) * HEAD_SIZE)
            qt, gt = q_ref[rows, cols], g_ref[rows, cols]
            for n, (piece, ref, first) in enumerate(((2, own_ref, blocks), (0, far_ref, 0))):
                parts = []
                for c, _, r in chunk_list(i, length, (piece,)):
                    s = masked_scores(c, ref[r : r + TILE, :width], qt, after)
                    dw = dot(ref[r : r + TILE, width:], gt, 1, 1)
                    parts.append((s, dw, bias_rows(docs, first + r // BLOCK, own_docs)))
                for k, value in enumerate(softmax_part(parts)):
                    at = (h * 2 + n) * 3 + k
                    stats_ref[at : at + 1, i * TILE : (i + 1) * TILE] = value


def outer_near_kernel(
    index_ref, q_ref, g_ref, own_ref, near_ref, part_ref, near_out, dq_out, stats_ref, acc_ref
):
    length = q_ref.shape[0] // 2
    width = own_ref.shape[1] // 2
    blocks = length // BLOCK
    base = lax.rem(index_ref[0], 2) * length
    docs = block_docs((near_ref, own_ref), length)
    far_bias = jnp.where(docs[blocks - 1] == 0.0, 0.0, NEG)
    key_t = jnp.transpose(near_ref[:length, :width])
    for i in range(length // TILE):
        own_docs = tile_docs(docs, blocks + i * (TILE // BLOCK))
        rows = pl.ds(pl.multiple_of(base + i * TILE, TILE), TILE)
        lanes = slice(i * TILE, (i + 1) * TILE)
        members = []
        chunks = chunk_list(i, length, (1,))
        for h in range(QUERY_PER_KEY):
            cols = slice(h * HEAD_SIZE, (h + 1) * HEAD_SIZE)
            qt, gt = q_ref[rows, cols], g_ref[rows, cols]
            at = h * 6
            own_top, own_total, own_mixed = [part_ref[at + k : at + k + 1, lanes] for k in range(3)]
            far_top, far_total, far_mixed = [
                part_ref[at + 3 + k : at + 4 + k, lanes] for k in range(3)
            ]
            top = jnp.maximum(own_top, far_top + far_bias)
            parts = []
            for c, _, r in chunks:
                s = dot(near_ref[r : r + TILE, :width], qt, 1, 1)
                dw = dot(near_ref[r : r + TILE, width:], gt, 1, 1)
                bias = bias_rows(docs, r // BLOCK, own_docs)
                top = chunk_top(s, bias, top)
                parts.append((s, dw, bias))
            shift = top * exponent_scale
            own_scale = jnp.exp2(own_top * exponent_scale - shift)
            far_scale = jnp.exp2(far_top * exponent_scale + (far_bias - shift))
            total = own_total * own_scale + far_total * far_scale
            mixed = own_mixed * own_scale + far_mixed * far_scale
            terms = []
            for s, dw, bias in parts:
                e = chunk_terms(s, bias, shift)
                terms.append(e)
                total = total + jnp.sum(e, axis=0, keepdims=True)
                mixed = mixed + jnp.sum(e * dw, axis=0, keepdims=True)
            inverse = 1.0 / total
            row_dot = mixed * inverse
            for k, value in enumerate((shift, inverse, row_dot)):
                stats_ref[h * 3 + k : h * 3 + k + 1, lanes] = value
            weights, dscores = [], []
            dq_t = jnp.zeros((width, TILE), jnp.float32)
            for e, (s, dw, bias), (c, _, r) in zip(terms, parts, chunks):
                w = e * inverse
                ds = (w * (dw - row_dot)).astype(jnp.bfloat16)
                weights.append(w.astype(jnp.bfloat16))
                dscores.append(ds)
                dq_t = dq_t + dot(key_t[:, r : r + TILE], ds, 1, 0)
            dq_out[h * width : (h + 1) * width, lanes] = dq_t
            members.append((qt, gt, weights, dscores))
        add_key_grads(acc_ref, members, [r for _, _, r in chunks], i == 0)
    near_out[...] = acc_ref[...].astype(jnp.bfloat16)


def add_key_grads(acc_ref, members, slots, first):
    width = acc_ref.shape[1] // 2
    q_all = jnp.concatenate([m[0] for m in members], axis=0)
    g_all = jnp.concatenate([m[1] for m in members], axis=0)
    for n, slot in enumerate(slots):
        w_all = jnp.concatenate([m[2][n] for m in members], axis=1)
        d_all = jnp.concatenate([m[3][n] for m in members], axis=1)
        dk = dot(d_all, q_all, 1, 0) * query_scaling
        dv = dot(w_all, g_all, 1, 0)
        at = slice(slot, slot + TILE)
        fresh = first if isinstance(first, bool) else slot in first
        if not fresh:
            dk = dk + acc_ref[at, :width]
            dv = dv + acc_ref[at, width:]
        acc_ref[at, :width] = dk
        acc_ref[at, width:] = dv


def outer_share_kernel(
    wanted, last, index_ref, q_ref, g_ref, own_ref, near_ref, far_ref, stats_ref, dq_part_ref, *refs
):
    length = q_ref.shape[0] // 2
    width = own_ref.shape[1] // 2
    blocks = length // BLOCK
    base = lax.rem(index_ref[0], 2) * length
    if wanted == 2:
        dq_in, dq_ref, grad_out, acc_ref = refs
    else:
        inner_far_ref, dq_ref, first_out, second_out, acc_ref = refs
    docs = block_docs((far_ref, near_ref, own_ref), length)
    after = triangle()
    piece = own_ref if wanted == 2 else far_ref
    key_t = jnp.transpose(piece[:length, :width])
    seen = set()
    for i in range(length // TILE):
        own_docs = tile_docs(docs, 2 * blocks + i * (TILE // BLOCK))
        rows = pl.ds(pl.multiple_of(base + i * TILE, TILE), TILE)
        lanes = slice(i * TILE, (i + 1) * TILE)
        members = []
        chunks = chunk_list(i, length, (wanted,))
        for h in range(QUERY_PER_KEY):
            cols = slice(h * HEAD_SIZE, (h + 1) * HEAD_SIZE)
            qt, gt = q_ref[rows, cols], g_ref[rows, cols]
            shift, inverse, row_dot = [
                stats_ref[h * 3 + k : h * 3 + k + 1, lanes] for k in range(3)
            ]
            weights, dscores = [], []
            dq_t = dq_part_ref[h * width : (h + 1) * width, lanes]
            for c, p, r in chunks:
                s = masked_scores(c, piece[r : r + TILE, :width], qt, after)
                dw = dot(piece[r : r + TILE, width:], gt, 1, 1)
                bias = bias_rows(docs, p * blocks + r // BLOCK, own_docs)
                w = chunk_terms(s, bias, shift) * inverse
                ds = (w * (dw - row_dot)).astype(jnp.bfloat16)
                weights.append(w.astype(jnp.bfloat16))
                dscores.append(ds)
                dq_t = dq_t + dot(key_t[:, r : r + TILE], ds, 1, 0)
            if wanted == 2:
                dq_ref[rows, cols] = jnp.transpose(dq_t * query_scaling).astype(jnp.bfloat16)
            else:
                dq_ref[h * width : (h + 1) * width, lanes] = dq_t
            members.append((qt, gt, weights, dscores))
        slots = [r for _, _, r in chunks]
        add_key_grads(acc_ref, members, slots, [x for x in slots if x not in seen])
        seen.update(slots)
    if wanted == 2:
        other = pl.ds(pl.multiple_of(length - base, length), length)
        for h in range(QUERY_PER_KEY):
            span = slice(h * width, (h + 1) * width)
            whole = jnp.transpose(dq_in[span, :] * query_scaling)
            dq_ref[other, span] = whole.astype(jnp.bfloat16)
        grad_out[...] = acc_ref[...]
    else:
        index = index_ref[0]
        _, _, even = halves(index)
        grad = acc_ref[...]
        grad = grad.astype(jnp.bfloat16)
        other = inner_far_ref[...]
        first_out[...] = jnp.where(even, other, grad)
        second_out[...] = jnp.where(even, grad, other)


def early_sum_kernel(last, index_ref, own, across, kept, out):
    grad = jnp.where(index_ref[0] == last, kept[...], across[...])
    out[...] = own[...] + grad.astype(jnp.float32)


def sum_kernel(
    index_ref, inner_own, outer_own, pair, first, second, dk_ref, dv_ref, held_ref, sems
):
    length = inner_own.shape[0]
    width = dk_ref.shape[1]
    inner, outer, even = halves(index_ref[0])
    f32 = jnp.float32
    one, two = first[...].astype(f32), second[...].astype(f32)
    copies = []
    for n, half in enumerate((inner, outer)):
        if n == 0:
            total = inner_own[...] + jnp.where(even, two, one)
        else:
            total = outer_own[...] + (pair[...].astype(f32) + jnp.where(even, one, two))
        rows = pl.ds(pl.multiple_of(half * length, length), length)
        for m, out in enumerate((dk_ref, dv_ref)):
            held_ref[2 * n + m] = total[:, m * width : (m + 1) * width].astype(jnp.bfloat16)
            copies.append(
                pltpu.make_async_copy(
                    held_ref.at[2 * n + m], out.at[rows, :], sems.at[2 * n + m]
                )
            )
            copies[-1].start()
    for copy in copies:
        copy.wait()


def smem():
    return pl.BlockSpec(memory_space=pltpu.SMEM)


def hbm():
    return pl.BlockSpec(memory_space=pltpu.HBM)


def vmem():
    return pl.BlockSpec(memory_space=pltpu.VMEM)


LIMIT = pltpu.CompilerParams(vmem_limit_bytes=16 * 1024 * 1024)
SMALL = pltpu.CompilerParams(vmem_limit_bytes=4 * 1024 * 1024)


def on_device(queries, keys, values, grad_out, starts):
    length = keys.shape[0] // 2
    width = keys.shape[1]
    count = lax.axis_size("seq")
    index = lax.axis_index("seq").astype(jnp.int32).reshape(1)
    assert count % 4 == 0
    last = count - 1
    pairs = [(d, d ^ 1) for d in range(count)]
    first = [(d, d ^ 2) for d in range(count)]
    second = [(d, ((d - 2) ^ 2) + 2) for d in range(2, count - 2)]
    across = [(d, d + 1 if d % 2 else d - 1) for d in range(1, last)]
    _, _, even = halves(index[0])

    bf16, f32 = jnp.bfloat16, jnp.float32
    narrow = jax.ShapeDtypeStruct((length, 2 * width), bf16)
    wide = jax.ShapeDtypeStruct((length, 2 * width), f32)
    rows = jax.ShapeDtypeStruct((16, length), f32)
    like_q = jax.ShapeDtypeStruct(queries.shape, bf16)
    unit = 2 * QUERY_PER_KEY * TILE * TILE * width

    def call(kernel, outs, operands, name, work, scratch=(), specs=None, limit=LIMIT, alias=None,
             out_specs=None):
        return pl.pallas_call(
            kernel,
            out_shape=outs,
            in_specs=specs or [smem()] + [vmem()] * (len(operands) - 1),
            out_specs=out_specs or (vmem(),) * len(outs),
            scratch_shapes=list(scratch),
            input_output_aliases=alias or {},
            compiler_params=limit,
            cost_estimate=pl.CostEstimate(
                flops=unit * work, bytes_accessed=1024 * 1024, transcendentals=0
            ),
            name=name,
        )(*operands)

    place = index[0]
    parity = lax.rem(place, 2)
    inner = pack_half(keys, values, starts, 1 - parity, place)
    outer = pack_half(keys, values, starts, parity, place)
    give_1 = jnp.where(even, outer, inner)
    give_2 = jnp.where(even, inner, outer)

    take_1 = lax.ppermute(give_1, "seq", first)
    heads = lax.axis_size("head")

    def spread(links):
        return [(a * heads + h, b * heads + h) for a, b in links for h in range(heads)]

    fold = [(last - 1, last), (last, last - 1)]
    ends = [(d * heads + h, d * heads + (h ^ 1)) for d in (0, 1) for h in range(heads)]
    take_2 = lax.ppermute(give_2, ("seq", "head"), spread(second + fold) + ends)
    inner_near = lax.ppermute(outer, "seq", pairs)
    inner_far = jnp.where(even, take_1, take_2)
    outer_far = jnp.where(even, take_2, take_1)
    q, g = queries, grad_out
    outer_near = lax.ppermute(inner_far, "seq", pairs)

    def after(value, *others):
        return lax.optimization_barrier((value,) + others)[0]

    grads = pltpu.VMEM((length, 2 * width), f32)
    dq_rows = jax.ShapeDtypeStruct((QUERY_PER_KEY * width, length), f32)

    (part,) = call(
        outer_stats_kernel, (rows,), (index, q, g, outer, outer_far), "outer_stats", 12
    )
    dq, inner_own, inner_g1, inner_g2 = call(
        inner_stage_kernel,
        (dq_rows, wide, narrow, narrow),
        (index, after(q, part), g, inner, inner_near, inner_far),
        "inner_stage",
        50,
        [pltpu.VMEM((3 * length, 2 * width), f32)],
    )
    pair_take = lax.ppermute(inner_g1, "seq", pairs)
    outer_g1, dq_part, stats = call(
        outer_near_kernel,
        (narrow, dq_rows, rows),
        (index, after(q, dq), g, outer, outer_near, part),
        "outer_near",
        20,
        [grads],
    )
    turns = [(d * heads + h, d * heads + (h ^ 1)) for d in (0, last) for h in range(heads)]
    inner_a = lax.ppermute(outer_g1, ("seq", "head"), spread(across) + turns)
    dq_part, give_1, give_2 = call(
        lambda *refs: outer_share_kernel(0, last, *refs),
        (dq_rows, narrow, narrow),
        (index, q, g, outer, outer_near, outer_far, stats, dq_part, inner_g2),
        "outer_far",
        15,
        [grads],
    )
    take_1 = lax.ppermute(give_1, "seq", first)
    take_2 = lax.ppermute(give_2, ("seq", "head"), spread(second + fold) + ends)
    dq, outer_own = call(
        lambda *refs: outer_share_kernel(2, last, *refs),
        (like_q, wide),
        (index, q, g, outer, outer_near, outer_far, stats, dq_part, dq),
        "outer_own",
        15,
        [grads],
    )
    (inner_own,) = call(
        lambda *refs: early_sum_kernel(last, *refs),
        (wide,),
        (index, inner_own, inner_a, outer_g1),
        "early_sum",
        0,
        limit=SMALL,
    )
    half = jax.ShapeDtypeStruct(keys.shape, bf16)
    dk, dv = call(
        sum_kernel,
        (half, half),
        (index, inner_own, outer_own, pair_take, take_1, take_2),
        "sum",
        1,
        [pltpu.VMEM((4, length, width), bf16), pltpu.SemaphoreType.DMA((4,))],
        limit=SMALL,
        out_specs=(hbm(),) * 2,
    )
    return dq, dk, dv


def solution(mesh):
    in_specs = (P("seq", "head"), P("seq", "head"), P("seq", "head"), P("seq", "head"), P("seq"))
    out_specs = (P("seq", "head"), P("seq", "head"), P("seq", "head"))
    return jax.shard_map(
        on_device, mesh=mesh, in_specs=in_specs, out_specs=out_specs, check_vma=False
    )
```

```python
import math

import jax
import jax.numpy as jnp
from jax import lax
from jax.experimental import pallas as pl
from jax.experimental.pallas import tpu as pltpu
from jax.sharding import PartitionSpec as P

HEAD_SIZE = 128
WINDOW = 1024
QUERY_PER_KEY = 2
BLOCK = 128
TILE = 256
MARK = 16
NEG = -1e30

query_scaling = 168.0 ** (-0.5)
exponent_scale = query_scaling * math.log2(math.e)


def dot(a, b, ca, cb):
    return lax.dot_general(a, b, (((ca,), (cb,)), ((), ())), preferred_element_type=jnp.float32)


def halves(index):
    parity = lax.rem(index, 2)
    even = lax.rem(parity + lax.div(index, 2), 2) == 0
    return 1 - parity, parity, even


def pack_half(keys, values, starts, half, place):
    length = keys.shape[0] // 2
    width = keys.shape[1]
    blocks = length // BLOCK
    both = [lax.dynamic_slice_in_dim(x, half * length, length, 0) for x in (keys, values)]
    starts = lax.optimization_barrier((starts, *both))[0]
    begins = lax.dynamic_slice_in_dim(starts, half * blocks, blocks, 0)
    first = (lax.iota(jnp.int32, blocks) == 0) & (place == 0) & (half == 0)
    begins = jnp.pad(jnp.where(first, 1, begins).astype(jnp.bfloat16), (0, MARK - blocks))
    marks = jnp.broadcast_to(begins[:, None], (MARK, 2 * width))
    return jnp.concatenate([jnp.concatenate(both, axis=1), marks], axis=0)


def block_docs(pieces, length):
    docs = []
    count = jnp.zeros((1, TILE), jnp.float32)
    for piece in pieces:
        marks = piece[length:, :TILE].astype(jnp.float32)
        for j in range(length // BLOCK):
            count = count + marks[j : j + 1, :]
            docs.append(count)
    return docs


def tile_docs(docs, first):
    lane = lax.broadcasted_iota(jnp.int32, (1, TILE), 1)
    own = docs[first]
    for b in range(1, TILE // BLOCK):
        own = jnp.where(lane >= b * BLOCK, docs[first + b], own)
    return own


def chunk_list(tile, length, wanted):
    found = []
    for c in range(WINDOW // TILE + 1):
        piece, row = divmod((tile + c) * TILE, length)
        if piece in wanted:
            found.append((c, piece, row))
    return found


def triangle():
    row = lax.broadcasted_iota(jnp.int32, (TILE, TILE), 0)
    return row > lax.broadcasted_iota(jnp.int32, (TILE, TILE), 1)


def masked_scores(c, keys, qt, after):
    s = dot(keys, qt, 1, 1)
    if c == 0:
        s = jnp.where(after, s, NEG)
    if c == WINDOW // TILE:
        s = jnp.where(after, NEG, s)
    return s


def bias_rows(docs, first, own):
    return [jnp.where(docs[first + b] == own, 0.0, NEG) for b in range(TILE // BLOCK)]


def chunk_top(s, bias, top):
    for b, row in enumerate(bias):
        t = jnp.max(s[b * BLOCK : (b + 1) * BLOCK], axis=0, keepdims=True) + row
        top = t if top is None else jnp.maximum(top, t)
    return top


def chunk_terms(s, bias, shift):
    return jnp.concatenate(
        [
            jnp.exp2(s[b * BLOCK : (b + 1) * BLOCK] * exponent_scale + (row - shift))
            for b, row in enumerate(bias)
        ],
        axis=0,
    )


def softmax_part(parts):
    top = None
    for s, dw, bias in parts:
        top = chunk_top(s, bias, top)
    shift = top * exponent_scale
    total = jnp.zeros((1, TILE), jnp.float32)
    mixed = jnp.zeros((1, TILE), jnp.float32)
    for s, dw, bias in parts:
        e = chunk_terms(s, bias, shift)
        total = total + jnp.sum(e, axis=0, keepdims=True)
        mixed = mixed + jnp.sum(e * dw, axis=0, keepdims=True)
    return top, total, mixed


def outer_stats_kernel(index_ref, q_ref, g_ref, own_ref, far_ref, stats_ref):
    length = q_ref.shape[0] // 2
    width = own_ref.shape[1] // 2
    blocks = length // BLOCK
    base = lax.rem(index_ref[0], 2) * length
    docs = block_docs((far_ref, own_ref), length)
    after = triangle()
    for i in range(length // TILE):
        own_docs = tile_docs(docs, blocks + i * (TILE // BLOCK))
        rows = pl.ds(pl.multiple_of(base + i * TILE, TILE), TILE)
        for h in range(QUERY_PER_KEY):
            cols = slice(h * HEAD_SIZE, (h + 1) * HEAD_SIZE)
            qt, gt = q_ref[rows, cols], g_ref[rows, cols]
            for n, (piece, ref, first) in enumerate(((2, own_ref, blocks), (0, far_ref, 0))):
                parts = []
                for c, _, r in chunk_list(i, length, (piece,)):
                    s = masked_scores(c, ref[r : r + TILE, :width], qt, after)
                    dw = dot(ref[r : r + TILE, width:], gt, 1, 1)
                    parts.append((s, dw, bias_rows(docs, first + r // BLOCK, own_docs)))
                for k, value in enumerate(softmax_part(parts)):
                    at = (h * 2 + n) * 3 + k
                    stats_ref[at : at + 1, i * TILE : (i + 1) * TILE] = value


def outer_near_kernel(
    index_ref, q_ref, g_ref, own_ref, near_ref, part_ref, near_out, dq_out, stats_ref, acc_ref
):
    length = q_ref.shape[0] // 2
    width = own_ref.shape[1] // 2
    blocks = length // BLOCK
    base = lax.rem(index_ref[0], 2) * length
    docs = block_docs((near_ref, own_ref), length)
    far_bias = jnp.where(docs[blocks - 1] == 0.0, 0.0, NEG)
    key_t = jnp.transpose(near_ref[:length, :width])
    steps = [(i, h) for i in range(length // TILE) for h in range(QUERY_PER_KEY)]

    def products(i, h):
        rows = pl.ds(pl.multiple_of(base + i * TILE, TILE), TILE)
        cols = slice(h * HEAD_SIZE, (h + 1) * HEAD_SIZE)
        qt, gt = q_ref[rows, cols], g_ref[rows, cols]
        own_docs = tile_docs(docs, blocks + i * (TILE // BLOCK))
        parts = []
        for c, _, r in chunk_list(i, length, (1,)):
            s = dot(near_ref[r : r + TILE, :width], qt, 1, 1)
            dw = dot(near_ref[r : r + TILE, width:], gt, 1, 1)
            parts.append((s, dw, bias_rows(docs, r // BLOCK, own_docs)))
        return qt, gt, parts

    def shares(i, h, parts):
        lanes = slice(i * TILE, (i + 1) * TILE)
        at = h * 6
        own_top, own_total, own_mixed = [part_ref[at + k : at + k + 1, lanes] for k in range(3)]
        far_top, far_total, far_mixed = [part_ref[at + 3 + k : at + 4 + k, lanes] for k in range(3)]
        top = jnp.maximum(own_top, far_top + far_bias)
        for s, dw, bias in parts:
            top = chunk_top(s, bias, top)
        shift = top * exponent_scale
        own_scale = jnp.exp2(own_top * exponent_scale - shift)
        far_scale = jnp.exp2(far_top * exponent_scale + (far_bias - shift))
        total = own_total * own_scale + far_total * far_scale
        mixed = own_mixed * own_scale + far_mixed * far_scale
        terms = []
        for s, dw, bias in parts:
            e = chunk_terms(s, bias, shift)
            terms.append(e)
            total = total + jnp.sum(e, axis=0, keepdims=True)
            mixed = mixed + jnp.sum(e * dw, axis=0, keepdims=True)
        inverse = 1.0 / total
        row_dot = mixed * inverse
        for k, value in enumerate((shift, inverse, row_dot)):
            stats_ref[h * 3 + k : h * 3 + k + 1, lanes] = value
        weights, dscores = [], []
        dq_t = jnp.zeros((width, TILE), jnp.float32)
        for e, (s, dw, bias), (c, _, r) in zip(terms, parts, chunk_list(i, length, (1,))):
            w = e * inverse
            ds = (w * (dw - row_dot)).astype(jnp.bfloat16)
            weights.append(w.astype(jnp.bfloat16))
            dscores.append(ds)
            dq_t = dq_t + dot(key_t[:, r : r + TILE], ds, 1, 0)
        dq_out[h * width : (h + 1) * width, lanes] = dq_t
        return weights, dscores

    members = []
    ready = products(*steps[0])
    for n, (i, h) in enumerate(steps):
        qt, gt, parts = ready
        if n + 1 < len(steps):
            ready = products(*steps[n + 1])
        members.append((qt, gt, *shares(i, h, parts)))
        if h == QUERY_PER_KEY - 1:
            slots = [r for _, _, r in chunk_list(i, length, (1,))]
            add_key_grads(acc_ref, members, slots, slots if i == 0 else [])
            members = []
    near_out[...] = acc_ref[...].astype(jnp.bfloat16)


def inner_stage_kernel(
    last, index_ref, q_ref, g_ref, own_ref, near_ref, far_ref, fold_ref,
    near_out, far_out, dq_out, stats_ref, acc_ref,
):
    length = q_ref.shape[0] // 2
    width = own_ref.shape[1] // 2
    blocks = length // BLOCK
    base = (1 - lax.rem(index_ref[0], 2)) * length
    pieces = (far_ref, near_ref, own_ref)
    docs = block_docs(pieces, length)
    after = triangle()
    key_t = [jnp.transpose(pieces[p][:length, :width]) for p in (0, 1)]
    steps = [(i, h) for i in range(length // TILE) for h in range(QUERY_PER_KEY)]

    def products(i, h):
        rows = pl.ds(pl.multiple_of(base + i * TILE, TILE), TILE)
        cols = slice(h * HEAD_SIZE, (h + 1) * HEAD_SIZE)
        qt, gt = q_ref[rows, cols], g_ref[rows, cols]
        own_docs = tile_docs(docs, 2 * blocks + i * (TILE // BLOCK))
        parts = []
        for c, p, r in chunk_list(i, length, (0, 1, 2)):
            s = masked_scores(c, pieces[p][r : r + TILE, :width], qt, after)
            dw = dot(pieces[p][r : r + TILE, width:], gt, 1, 1)
            parts.append((s, dw, bias_rows(docs, p * blocks + r // BLOCK, own_docs)))
        return qt, gt, parts

    def shares(i, h, parts):
        lanes = slice(i * TILE, (i + 1) * TILE)
        top = None
        for s, dw, bias in parts:
            top = chunk_top(s, bias, top)
        shift = top * exponent_scale
        total = jnp.zeros((1, TILE), jnp.float32)
        mixed = jnp.zeros((1, TILE), jnp.float32)
        terms = []
        for s, dw, bias in parts:
            e = chunk_terms(s, bias, shift)
            terms.append(e)
            total = total + jnp.sum(e, axis=0, keepdims=True)
            mixed = mixed + jnp.sum(e * dw, axis=0, keepdims=True)
        inverse = 1.0 / total
        row_dot = mixed * inverse
        for k, value in enumerate((shift, inverse, row_dot)):
            stats_ref[h * 3 + k : h * 3 + k + 1, lanes] = value
        weights, dscores = [], []
        dq_t = jnp.zeros((width, TILE), jnp.float32)
        for e, (s, dw, bias), (c, p, r) in zip(terms, parts, chunk_list(i, length, (0, 1, 2))):
            if p == 2:
                continue
            w = e * inverse
            ds = (w * (dw - row_dot)).astype(jnp.bfloat16)
            weights.append(w.astype(jnp.bfloat16))
            dscores.append(ds)
            dq_t = dq_t + dot(key_t[p][:, r : r + TILE], ds, 1, 0)
        dq_out[h * width : (h + 1) * width, lanes] = dq_t
        return weights, dscores

    seen = set()
    members = []
    ready = products(*steps[0])
    for n, (i, h) in enumerate(steps):
        qt, gt, parts = ready
        if n + 1 < len(steps):
            ready = products(*steps[n + 1])
        members.append((qt, gt, *shares(i, h, parts)))
        if h == QUERY_PER_KEY - 1:
            slots = [p * length + r for _, p, r in chunk_list(i, length, (0, 1))]
            add_key_grads(acc_ref, members, slots, [x for x in slots if x not in seen])
            seen.update(slots)
            members = []
    more = jnp.where(index_ref[0] == last, fold_ref[...].astype(jnp.float32), 0.0)
    near_out[...] = (acc_ref[length:] + more).astype(jnp.bfloat16)
    far_out[...] = acc_ref[:length].astype(jnp.bfloat16)


def add_key_grads(acc_ref, members, slots, first):
    width = acc_ref.shape[1] // 2
    q_all = jnp.concatenate([m[0] for m in members], axis=0)
    g_all = jnp.concatenate([m[1] for m in members], axis=0)
    for n, slot in enumerate(slots):
        w_all = jnp.concatenate([m[2][n] for m in members], axis=1)
        d_all = jnp.concatenate([m[3][n] for m in members], axis=1)
        dk = dot(d_all, q_all, 1, 0) * query_scaling
        dv = dot(w_all, g_all, 1, 0)
        at = slice(slot, slot + TILE)
        fresh = first if isinstance(first, bool) else slot in first
        if not fresh:
            dk = dk + acc_ref[at, :width]
            dv = dv + acc_ref[at, width:]
        acc_ref[at, :width] = dk
        acc_ref[at, width:] = dv


def outer_far_share(
    index_ref, q_ref, g_ref, own_ref, near_ref, far_ref, stats_ref, dq_part_ref, dq_ref, acc_ref
):
    length = q_ref.shape[0] // 2
    width = own_ref.shape[1] // 2
    base = lax.rem(index_ref[0], 2) * length
    docs = block_docs((far_ref, near_ref, own_ref), length)
    key_t = jnp.transpose(far_ref[:length, :width])
    piece_share(
        0, 0, base, docs, 2 * (length // BLOCK), triangle(), key_t, q_ref, g_ref, far_ref,
        stats_ref, dq_part_ref, dq_ref, acc_ref,
    )


def outer_far_kernel(
    last, index_ref, q_ref, g_ref, own_ref, near_ref, far_ref, stats_ref, dq_part_ref,
    inner_far_ref, dq_ref, first_out, second_out, acc_ref,
):
    @pl.when(index_ref[0] != last)
    def _():
        outer_far_share(
            index_ref, q_ref, g_ref, own_ref, near_ref, far_ref, stats_ref, dq_part_ref, dq_ref,
            acc_ref,
        )

    @pl.when(index_ref[0] == last)
    def _():
        dq_ref[...] = dq_part_ref[...]
        acc_ref[...] = jnp.zeros_like(acc_ref)

    _, _, even = halves(index_ref[0])
    grad = acc_ref[...].astype(jnp.bfloat16)
    other = inner_far_ref[...]
    first_out[...] = jnp.where(even, other, grad)
    second_out[...] = jnp.where(even, grad, other)


def piece_share(
    piece, first, base, docs, places, after, key_t, q_ref, g_ref, piece_ref,
    stats_ref, dq_part_ref, dq_ref, acc_ref,
):
    length, width = q_ref.shape[0] // 2, piece_ref.shape[1] // 2
    steps = [(i, h) for i in range(length // TILE) for h in range(QUERY_PER_KEY)]

    def products(i, h):
        rows = pl.ds(pl.multiple_of(base + i * TILE, TILE), TILE)
        cols = slice(h * HEAD_SIZE, (h + 1) * HEAD_SIZE)
        qt, gt = q_ref[rows, cols], g_ref[rows, cols]
        own_docs = tile_docs(docs, places + i * (TILE // BLOCK))
        parts = []
        for c, _, r in chunk_list(i, length, (piece,)):
            s = masked_scores(c, piece_ref[r : r + TILE, :width], qt, after)
            dw = dot(piece_ref[r : r + TILE, width:], gt, 1, 1)
            parts.append((s, dw, bias_rows(docs, first + r // BLOCK, own_docs), r))
        return qt, gt, parts

    seen = set()
    members = []
    ready = products(*steps[0])
    for n, (i, h) in enumerate(steps):
        qt, gt, parts = ready
        if n + 1 < len(steps):
            ready = products(*steps[n + 1])
        lanes = slice(i * TILE, (i + 1) * TILE)
        shift, inverse, row_dot = [stats_ref[h * 3 + k : h * 3 + k + 1, lanes] for k in range(3)]
        weights, dscores = [], []
        dq_t = dq_part_ref[h * width : (h + 1) * width, lanes]
        for s, dw, bias, r in parts:
            w = chunk_terms(s, bias, shift) * inverse
            ds = (w * (dw - row_dot)).astype(jnp.bfloat16)
            weights.append(w.astype(jnp.bfloat16))
            dscores.append(ds)
            dq_t = dq_t + dot(key_t[:, r : r + TILE], ds, 1, 0)
        if piece == 2:
            rows = pl.ds(pl.multiple_of(base + i * TILE, TILE), TILE)
            cols = slice(h * HEAD_SIZE, (h + 1) * HEAD_SIZE)
            dq_ref[rows, cols] = jnp.transpose(dq_t * query_scaling).astype(jnp.bfloat16)
        else:
            dq_ref[h * width : (h + 1) * width, lanes] = dq_t
        members.append((qt, gt, weights, dscores))
        if h == QUERY_PER_KEY - 1:
            slots = [r for _, _, _, r in parts]
            add_key_grads(acc_ref, members, slots, [x for x in slots if x not in seen])
            seen.update(slots)
            members = []


def own_kernel(
    index_ref, q_ref, g_ref, inner_ref, inner_stats, inner_dq, outer_ref, outer_stats, outer_dq,
    dq_ref, inner_out, outer_out,
):
    length = q_ref.shape[0] // 2
    width = inner_ref.shape[1] // 2
    parity = lax.rem(index_ref[0], 2)
    after = triangle()
    for half, own_ref, stats_ref, dq_part_ref, out_ref in (
        (1 - parity, inner_ref, inner_stats, inner_dq, inner_out),
        (parity, outer_ref, outer_stats, outer_dq, outer_out),
    ):
        docs = block_docs((own_ref,), length)
        key_t = jnp.transpose(own_ref[:length, :width])
        piece_share(
            2, 0, half * length, docs, 0, after, key_t, q_ref, g_ref, own_ref,
            stats_ref, dq_part_ref, dq_ref, out_ref,
        )


def fold_kernel(
    last, index_ref, q_ref, g_ref, own_ref, near_ref, far_ref, part_ref,
    near_out, far_out, dq_out, stats_ref, dq_ref, acc_ref,
):
    @pl.when(index_ref[0] == last)
    def _():
        outer_near_kernel(
            index_ref, q_ref, g_ref, own_ref, near_ref, part_ref, near_out, dq_ref, stats_ref,
            acc_ref,
        )
        outer_far_share(
            index_ref, q_ref, g_ref, own_ref, near_ref, far_ref, stats_ref, dq_ref, dq_out, acc_ref
        )
        far_out[...] = acc_ref[...].astype(jnp.bfloat16)


def near_kernel(
    last, index_ref, q_ref, g_ref, own_ref, near_ref, part_ref, fold_near, fold_dq, fold_stats,
    near_out, dq_out, stats_ref, acc_ref,
):
    @pl.when(index_ref[0] != last)
    def _():
        outer_near_kernel(
            index_ref, q_ref, g_ref, own_ref, near_ref, part_ref, near_out, dq_out, stats_ref,
            acc_ref,
        )

    @pl.when(index_ref[0] == last)
    def _():
        near_out[...] = fold_near[...]
        dq_out[...] = fold_dq[...]
        stats_ref[...] = fold_stats[...]


def early_sum_kernel(last, index_ref, own, across, kept, out):
    grad = jnp.where(index_ref[0] == last, kept[...], across[...])
    out[...] = own[...] + grad.astype(jnp.float32)


def sum_kernel(
    index_ref, inner_own, outer_own, pair, first, second, dk_ref, dv_ref, held_ref, sems
):
    length = inner_own.shape[0]
    width = dk_ref.shape[1]
    inner, outer, even = halves(index_ref[0])
    f32 = jnp.float32
    one, two = first[...].astype(f32), second[...].astype(f32)
    copies = []
    for n, half in enumerate((inner, outer)):
        if n == 0:
            total = inner_own[...] + jnp.where(even, two, one)
        else:
            total = outer_own[...] + (pair[...].astype(f32) + jnp.where(even, one, two))
        rows = pl.ds(pl.multiple_of(half * length, length), length)
        for m, out in enumerate((dk_ref, dv_ref)):
            held_ref[2 * n + m] = total[:, m * width : (m + 1) * width].astype(jnp.bfloat16)
            copies.append(
                pltpu.make_async_copy(
                    held_ref.at[2 * n + m], out.at[rows, :], sems.at[2 * n + m]
                )
            )
            copies[-1].start()
    for copy in copies:
        copy.wait()


def smem():
    return pl.BlockSpec(memory_space=pltpu.SMEM)


def hbm():
    return pl.BlockSpec(memory_space=pltpu.HBM)


def vmem():
    return pl.BlockSpec(memory_space=pltpu.VMEM)


LIMIT = pltpu.CompilerParams(vmem_limit_bytes=16 * 1024 * 1024)
SMALL = pltpu.CompilerParams(vmem_limit_bytes=4 * 1024 * 1024)


def on_device(queries, keys, values, grad_out, starts):
    length = keys.shape[0] // 2
    width = keys.shape[1]
    count = lax.axis_size("seq")
    index = lax.axis_index("seq").astype(jnp.int32).reshape(1)
    assert count % 4 == 0
    last = count - 1
    pairs = [(d, d ^ 1) for d in range(count)]
    first = [(d, d ^ 2) for d in range(count)]
    second = [(d, ((d - 2) ^ 2) + 2) for d in range(2, count - 2)]
    across = [(d, d + 1 if d % 2 else d - 1) for d in range(1, last)]
    _, _, even = halves(index[0])

    bf16, f32 = jnp.bfloat16, jnp.float32
    narrow = jax.ShapeDtypeStruct((length, 2 * width), bf16)
    wide = jax.ShapeDtypeStruct((length, 2 * width), f32)
    rows = jax.ShapeDtypeStruct((16, length), f32)
    like_q = jax.ShapeDtypeStruct(queries.shape, bf16)
    unit = 2 * QUERY_PER_KEY * TILE * TILE * width

    def call(kernel, outs, operands, name, work, scratch=(), specs=None, limit=LIMIT, alias=None,
             out_specs=None):
        return pl.pallas_call(
            kernel,
            out_shape=outs,
            in_specs=specs or [smem()] + [vmem()] * (len(operands) - 1),
            out_specs=out_specs or (vmem(),) * len(outs),
            scratch_shapes=list(scratch),
            input_output_aliases=alias or {},
            compiler_params=limit,
            cost_estimate=pl.CostEstimate(
                flops=unit * work, bytes_accessed=1024 * 1024, transcendentals=0
            ),
            name=name,
        )(*operands)

    place = index[0]
    parity = lax.rem(place, 2)
    inner = pack_half(keys, values, starts, 1 - parity, place)
    outer = pack_half(keys, values, starts, parity, place)
    give_1 = jnp.where(even, outer, inner)
    give_2 = jnp.where(even, inner, outer)

    take_1 = lax.ppermute(give_1, "seq", first)
    heads = lax.axis_size("head")

    def spread(links):
        return [(a * heads + h, b * heads + h) for a, b in links for h in range(heads)]

    fold = [(last - 1, last), (last, last - 1)]
    ends = [(d * heads + h, d * heads + (h ^ 1)) for d in (0, 1) for h in range(heads)]
    take_2 = lax.ppermute(give_2, ("seq", "head"), spread(second + fold) + ends)
    inner_near = lax.ppermute(outer, "seq", pairs)
    inner_far = jnp.where(even, take_1, take_2)
    outer_far = jnp.where(even, take_2, take_1)
    q, g = queries, grad_out
    outer_near = lax.ppermute(inner_far, "seq", pairs)

    def after(value, *others):
        return lax.optimization_barrier((value,) + others)[0]

    grads = pltpu.VMEM((length, 2 * width), f32)
    dq_rows = jax.ShapeDtypeStruct((QUERY_PER_KEY * width, length), f32)

    (part,) = call(
        outer_stats_kernel, (rows,), (index, q, g, outer, outer_far), "outer_stats", 12
    )
    fold_near, fold_far, fold_dq, fold_stats = call(
        lambda *refs: fold_kernel(last, *refs),
        (narrow, narrow, dq_rows, rows),
        (index, q, g, outer, inner, outer_far, part),
        "fold",
        1,
        [pltpu.VMEM(dq_rows.shape, f32), grads],
    )
    inner_g1, inner_g2, inner_dq, inner_stats = call(
        lambda *refs: inner_stage_kernel(last, *refs),
        (narrow, narrow, dq_rows, rows),
        (index, q, g, inner, inner_near, inner_far, fold_far),
        "inner_stage",
        40,
        [pltpu.VMEM((2 * length, 2 * width), f32)],
    )
    pair_take = lax.ppermute(inner_g1, "seq", pairs)
    outer_g1, dq_part, stats = call(
        lambda *refs: near_kernel(last, *refs),
        (narrow, dq_rows, rows),
        (index, after(q, inner_g1), g, outer, outer_near, part, fold_near, fold_dq, fold_stats),
        "outer_near",
        20,
        [grads],
    )
    turns = [(d * heads + h, d * heads + (h ^ 1)) for d in (0, last) for h in range(heads)]
    inner_a = lax.ppermute(outer_g1, ("seq", "head"), spread(across) + turns)
    dq_part, give_1, give_2 = call(
        lambda *refs: outer_far_kernel(last, *refs),
        (dq_rows, narrow, narrow),
        (index, q, g, outer, outer_near, outer_far, stats, dq_part, inner_g2),
        "outer_far",
        15,
        [grads],
    )
    take_1 = lax.ppermute(give_1, "seq", first)
    take_2 = lax.ppermute(give_2, ("seq", "head"), spread(second + fold[:1]) + ends)
    dq, inner_own, outer_own = call(
        own_kernel,
        (like_q, wide, wide),
        (index, q, g, inner, inner_stats, inner_dq, outer, stats, dq_part),
        "own",
        30,
    )
    (inner_own,) = call(
        lambda *refs: early_sum_kernel(last, *refs),
        (wide,),
        (index, inner_own, inner_a, outer_g1),
        "early_sum",
        0,
        limit=SMALL,
    )
    half = jax.ShapeDtypeStruct(keys.shape, bf16)
    dk, dv = call(
        sum_kernel,
        (half, half),
        (index, inner_own, outer_own, pair_take, take_1, take_2),
        "sum",
        1,
        [pltpu.VMEM((4, length, width), bf16), pltpu.SemaphoreType.DMA((4,))],
        limit=SMALL,
        out_specs=(hbm(),) * 2,
    )
    return dq, dk, dv


def solution(mesh):
    in_specs = (P("seq", "head"), P("seq", "head"), P("seq", "head"), P("seq", "head"), P("seq"))
    out_specs = (P("seq", "head"), P("seq", "head"), P("seq", "head"))
    return jax.shard_map(
        on_device, mesh=mesh, in_specs=in_specs, out_specs=out_specs, check_vma=False
    )
```

```python
import math

import jax
import jax.numpy as jnp
from jax import lax
from jax.experimental import pallas as pl
from jax.experimental.pallas import tpu as pltpu
from jax.sharding import PartitionSpec as P

HEAD_SIZE = 128
WINDOW = 1024
QUERY_PER_KEY = 2
BLOCK = 128
TILE = 256
MARK = 16
NEG = -1e30

query_scaling = 168.0 ** (-0.5)
exponent_scale = query_scaling * math.log2(math.e)


def dot(a, b, ca, cb):
    return lax.dot_general(a, b, (((ca,), (cb,)), ((), ())), preferred_element_type=jnp.float32)


def halves(index):
    parity = lax.rem(index, 2)
    even = lax.rem(parity + lax.div(index, 2), 2) == 0
    return 1 - parity, parity, even


def pack_halves(keys, values, starts, parity, place):
    length = keys.shape[0] // 2
    blocks = length // BLOCK
    halves = (1 - parity, parity)
    parts = [
        lax.dynamic_slice_in_dim(x, half * length, length, 0)
        for half in halves
        for x in (keys, values)
    ]
    begins = [starts[:blocks], starts[blocks:]]
    first = (lax.iota(jnp.int32, blocks) == 0) & (place == 0)
    begins[0] = jnp.where(first, 1, begins[0])
    packs = []
    for n, half in enumerate(halves):
        rows = jnp.where(half == 0, begins[0], begins[1]).astype(jnp.bfloat16)
        rows = jnp.pad(rows, (0, MARK - blocks))
        marks = jnp.broadcast_to(rows[:, None], (MARK, 2 * keys.shape[1]))
        both = jnp.concatenate(parts[2 * n : 2 * n + 2], axis=1)
        packs.append(jnp.concatenate([both, marks], axis=0))
    return packs


def block_docs(pieces, length):
    docs = []
    count = jnp.zeros((1, TILE), jnp.float32)
    for piece in pieces:
        marks = piece[length:, :TILE].astype(jnp.float32)
        for j in range(length // BLOCK):
            count = count + marks[j : j + 1, :]
            docs.append(count)
    return docs


def tile_docs(docs, first):
    lane = lax.broadcasted_iota(jnp.int32, (1, TILE), 1)
    own = docs[first]
    for b in range(1, TILE // BLOCK):
        own = jnp.where(lane >= b * BLOCK, docs[first + b], own)
    return own


def chunk_list(tile, length, wanted):
    found = []
    for c in range(WINDOW // TILE + 1):
        piece, row = divmod((tile + c) * TILE, length)
        if piece in wanted:
            found.append((c, piece, row))
    return found


def triangle():
    row = lax.broadcasted_iota(jnp.int32, (TILE, TILE), 0)
    return row > lax.broadcasted_iota(jnp.int32, (TILE, TILE), 1)


def spans(chunks):
    runs = []
    for chunk in chunks:
        if runs and runs[-1][-1][1] == chunk[1]:
            runs[-1].append(chunk)
        else:
            runs.append([chunk])
    return runs


def run_products(run, piece_ref, qt, gt, after):
    width = piece_ref.shape[1] // 2
    rows = slice(run[0][2], run[0][2] + len(run) * TILE)
    scores = dot(piece_ref[rows, :width], qt, 1, 1)
    dweights = dot(piece_ref[rows, width:], gt, 1, 1)
    found = []
    for n, (c, _, _) in enumerate(run):
        s = scores[n * TILE : (n + 1) * TILE]
        if c == 0:
            s = jnp.where(after, s, NEG)
        if c == WINDOW // TILE:
            s = jnp.where(after, NEG, s)
        found.append((s, dweights[n * TILE : (n + 1) * TILE]))
    return found


def query_share(key_t, runs, dscores):
    total = None
    n = 0
    for run in runs:
        p, r = run[0][1:]
        ds = jnp.concatenate(dscores[n : n + len(run)], axis=0)
        n += len(run)
        part = dot(key_t[p][:, r : r + ds.shape[0]], ds, 1, 0)
        total = part if total is None else total + part
    return total


def bias_rows(docs, first, own):
    return [jnp.where(docs[first + b] == own, 0.0, NEG) for b in range(TILE // BLOCK)]


def chunk_top(s, bias, top):
    for b, row in enumerate(bias):
        t = jnp.max(s[b * BLOCK : (b + 1) * BLOCK], axis=0, keepdims=True) + row
        top = t if top is None else jnp.maximum(top, t)
    return top


def chunk_terms(s, bias, shift):
    return jnp.concatenate(
        [
            jnp.exp2(s[b * BLOCK : (b + 1) * BLOCK] * exponent_scale + (row - shift))
            for b, row in enumerate(bias)
        ],
        axis=0,
    )


def softmax_part(parts):
    top = None
    for s, dw, bias in parts:
        top = chunk_top(s, bias, top)
    shift = top * exponent_scale
    total = jnp.zeros((1, TILE), jnp.float32)
    mixed = jnp.zeros((1, TILE), jnp.float32)
    for s, dw, bias in parts:
        e = chunk_terms(s, bias, shift)
        total = total + jnp.sum(e, axis=0, keepdims=True)
        mixed = mixed + jnp.sum(e * dw, axis=0, keepdims=True)
    return top, total, mixed


def outer_stats_kernel(index_ref, q_ref, g_ref, own_ref, far_ref, stats_ref):
    length = q_ref.shape[0] // 2
    width = own_ref.shape[1] // 2
    blocks = length // BLOCK
    base = lax.rem(index_ref[0], 2) * length
    docs = block_docs((far_ref, own_ref), length)
    after = triangle()
    for i in range(length // TILE):
        own_docs = tile_docs(docs, blocks + i * (TILE // BLOCK))
        rows = pl.ds(pl.multiple_of(base + i * TILE, TILE), TILE)
        for h in range(QUERY_PER_KEY):
            cols = slice(h * HEAD_SIZE, (h + 1) * HEAD_SIZE)
            qt, gt = q_ref[rows, cols], g_ref[rows, cols]
            for n, (piece, ref, first) in enumerate(((2, own_ref, blocks), (0, far_ref, 0))):
                parts = []
                for run in spans(chunk_list(i, length, (piece,))):
                    for (_, _, r), (s, dw) in zip(run, run_products(run, ref, qt, gt, after)):
                        parts.append((s, dw, bias_rows(docs, first + r // BLOCK, own_docs)))
                for k, value in enumerate(softmax_part(parts)):
                    at = (h * 2 + n) * 3 + k
                    stats_ref[at : at + 1, i * TILE : (i + 1) * TILE] = value


def outer_near_kernel(
    index_ref, q_ref, g_ref, own_ref, near_ref, part_ref, near_out, dq_out, stats_ref, acc_ref
):
    length = q_ref.shape[0] // 2
    width = own_ref.shape[1] // 2
    blocks = length // BLOCK
    base = lax.rem(index_ref[0], 2) * length
    docs = block_docs((near_ref, own_ref), length)
    far_bias = jnp.where(docs[blocks - 1] == 0.0, 0.0, NEG)
    key_t = jnp.transpose(near_ref[:length, :width])
    steps = [(i, h) for i in range(length // TILE) for h in range(QUERY_PER_KEY)]

    def products(i, h):
        rows = pl.ds(pl.multiple_of(base + i * TILE, TILE), TILE)
        cols = slice(h * HEAD_SIZE, (h + 1) * HEAD_SIZE)
        qt, gt = q_ref[rows, cols], g_ref[rows, cols]
        own_docs = tile_docs(docs, blocks + i * (TILE // BLOCK))
        parts = []
        for run in spans(chunk_list(i, length, (1,))):
            for (_, _, r), (s, dw) in zip(run, run_products(run, near_ref, qt, gt, None)):
                parts.append((s, dw, bias_rows(docs, r // BLOCK, own_docs)))
        return qt, gt, parts

    def shares(i, h, parts):
        lanes = slice(i * TILE, (i + 1) * TILE)
        at = h * 6
        own_top, own_total, own_mixed = [part_ref[at + k : at + k + 1, lanes] for k in range(3)]
        far_top, far_total, far_mixed = [part_ref[at + 3 + k : at + 4 + k, lanes] for k in range(3)]
        top = jnp.maximum(own_top, far_top + far_bias)
        for s, dw, bias in parts:
            top = chunk_top(s, bias, top)
        shift = top * exponent_scale
        own_scale = jnp.exp2(own_top * exponent_scale - shift)
        far_scale = jnp.exp2(far_top * exponent_scale + (far_bias - shift))
        total = own_total * own_scale + far_total * far_scale
        mixed = own_mixed * own_scale + far_mixed * far_scale
        terms = []
        for s, dw, bias in parts:
            e = chunk_terms(s, bias, shift)
            terms.append(e)
            total = total + jnp.sum(e, axis=0, keepdims=True)
            mixed = mixed + jnp.sum(e * dw, axis=0, keepdims=True)
        inverse = 1.0 / total
        row_dot = mixed * inverse
        for k, value in enumerate((shift, inverse, row_dot)):
            stats_ref[h * 3 + k : h * 3 + k + 1, lanes] = value
        weights, dscores = [], []
        for e, (s, dw, bias) in zip(terms, parts):
            w = e * inverse
            dscores.append((w * (dw - row_dot)).astype(jnp.bfloat16))
            weights.append(w.astype(jnp.bfloat16))
        dq_out[h * width : (h + 1) * width, lanes] = query_share(
            {1: key_t}, spans(chunk_list(i, length, (1,))), dscores
        )
        return weights, dscores

    members = []
    ready = products(*steps[0])
    for n, (i, h) in enumerate(steps):
        qt, gt, parts = ready
        if n + 1 < len(steps):
            ready = products(*steps[n + 1])
        members.append((qt, gt, *shares(i, h, parts)))
        if h == QUERY_PER_KEY - 1:
            slots = [r for _, _, r in chunk_list(i, length, (1,))]
            add_key_grads(acc_ref, members, slots, slots if i == 0 else [])
            members = []
    near_out[...] = acc_ref[...].astype(jnp.bfloat16)


def inner_stage_kernel(
    last, index_ref, q_ref, g_ref, own_ref, near_ref, far_ref, fold_ref,
    near_out, far_out, dq_out, stats_ref, acc_ref,
):
    length = q_ref.shape[0] // 2
    width = own_ref.shape[1] // 2
    blocks = length // BLOCK
    base = (1 - lax.rem(index_ref[0], 2)) * length
    pieces = (far_ref, near_ref, own_ref)
    docs = block_docs(pieces, length)
    after = triangle()
    key_t = [jnp.transpose(pieces[p][:length, :width]) for p in (0, 1)]
    steps = [(i, h) for i in range(length // TILE) for h in range(QUERY_PER_KEY)]

    def products(i, h):
        rows = pl.ds(pl.multiple_of(base + i * TILE, TILE), TILE)
        cols = slice(h * HEAD_SIZE, (h + 1) * HEAD_SIZE)
        qt, gt = q_ref[rows, cols], g_ref[rows, cols]
        own_docs = tile_docs(docs, 2 * blocks + i * (TILE // BLOCK))
        parts = []
        for run in spans(chunk_list(i, length, (0, 1, 2))):
            found = run_products(run, pieces[run[0][1]], qt, gt, after)
            for (_, p, r), (s, dw) in zip(run, found):
                parts.append((s, dw, bias_rows(docs, p * blocks + r // BLOCK, own_docs)))
        return qt, gt, parts

    def shares(i, h, parts):
        lanes = slice(i * TILE, (i + 1) * TILE)
        top = None
        for s, dw, bias in parts:
            top = chunk_top(s, bias, top)
        shift = top * exponent_scale
        total = jnp.zeros((1, TILE), jnp.float32)
        mixed = jnp.zeros((1, TILE), jnp.float32)
        terms = []
        for s, dw, bias in parts:
            e = chunk_terms(s, bias, shift)
            terms.append(e)
            total = total + jnp.sum(e, axis=0, keepdims=True)
            mixed = mixed + jnp.sum(e * dw, axis=0, keepdims=True)
        inverse = 1.0 / total
        row_dot = mixed * inverse
        for k, value in enumerate((shift, inverse, row_dot)):
            stats_ref[h * 3 + k : h * 3 + k + 1, lanes] = value
        weights, dscores = [], []
        for e, (s, dw, bias), (c, p, r) in zip(terms, parts, chunk_list(i, length, (0, 1, 2))):
            if p == 2:
                continue
            w = e * inverse
            dscores.append((w * (dw - row_dot)).astype(jnp.bfloat16))
            weights.append(w.astype(jnp.bfloat16))
        dq_out[h * width : (h + 1) * width, lanes] = query_share(
            key_t, spans(chunk_list(i, length, (0, 1))), dscores
        )
        return weights, dscores

    seen = set()
    members = []
    ready = products(*steps[0])
    for n, (i, h) in enumerate(steps):
        qt, gt, parts = ready
        if n + 1 < len(steps):
            ready = products(*steps[n + 1])
        members.append((qt, gt, *shares(i, h, parts)))
        if h == QUERY_PER_KEY - 1:
            slots = [p * length + r for _, p, r in chunk_list(i, length, (0, 1))]
            add_key_grads(acc_ref, members, slots, [x for x in slots if x not in seen])
            seen.update(slots)
            members = []
    more = jnp.where(index_ref[0] == last, fold_ref[...].astype(jnp.float32), 0.0)
    near_out[...] = (acc_ref[length:] + more).astype(jnp.bfloat16)
    far_out[...] = acc_ref[:length].astype(jnp.bfloat16)


def add_key_grads(acc_ref, members, slots, first):
    width = acc_ref.shape[1] // 2
    q_all = jnp.concatenate([m[0] for m in members], axis=0)
    g_all = jnp.concatenate([m[1] for m in members], axis=0)
    n = 0
    while n < len(slots):
        m = n + 1
        while m < len(slots) and slots[m] == slots[m - 1] + TILE and m - n < 2:
            m += 1
        w_all, d_all = [
            jnp.concatenate(
                [jnp.concatenate([x[k][c] for x in members], axis=1) for c in range(n, m)], axis=0
            )
            for k in (2, 3)
        ]
        dk = dot(d_all, q_all, 1, 0) * query_scaling
        dv = dot(w_all, g_all, 1, 0)
        for c in range(n, m):
            at = slice(slots[c], slots[c] + TILE)
            own = slice((c - n) * TILE, (c - n + 1) * TILE)
            if (first is True) or (first is not False and slots[c] in first):
                acc_ref[at, :width] = dk[own]
                acc_ref[at, width:] = dv[own]
            else:
                acc_ref[at, :width] = acc_ref[at, :width] + dk[own]
                acc_ref[at, width:] = acc_ref[at, width:] + dv[own]
        n = m


def outer_far_share(
    index_ref, q_ref, g_ref, own_ref, near_ref, far_ref, stats_ref, dq_part_ref, dq_ref, acc_ref
):
    length = q_ref.shape[0] // 2
    width = own_ref.shape[1] // 2
    base = lax.rem(index_ref[0], 2) * length
    docs = block_docs((far_ref, near_ref, own_ref), length)
    key_t = jnp.transpose(far_ref[:length, :width])
    piece_share(
        0, 0, base, docs, 2 * (length // BLOCK), triangle(), key_t, q_ref, g_ref, far_ref,
        stats_ref, dq_part_ref, dq_ref, acc_ref,
    )


def outer_far_kernel(
    last, index_ref, q_ref, g_ref, own_ref, near_ref, far_ref, stats_ref, dq_part_ref,
    inner_far_ref, dq_ref, first_out, second_out, acc_ref,
):
    @pl.when(index_ref[0] != last)
    def _():
        outer_far_share(
            index_ref, q_ref, g_ref, own_ref, near_ref, far_ref, stats_ref, dq_part_ref, dq_ref,
            acc_ref,
        )

    @pl.when(index_ref[0] == last)
    def _():
        dq_ref[...] = dq_part_ref[...]
        acc_ref[...] = jnp.zeros_like(acc_ref)

    _, _, even = halves(index_ref[0])
    grad = acc_ref[...].astype(jnp.bfloat16)
    other = inner_far_ref[...]
    first_out[...] = jnp.where(even, other, grad)
    second_out[...] = jnp.where(even, grad, other)


def piece_share(
    piece, first, base, docs, places, after, key_t, q_ref, g_ref, piece_ref,
    stats_ref, dq_part_ref, dq_ref, acc_ref,
):
    length, width = q_ref.shape[0] // 2, piece_ref.shape[1] // 2
    steps = [(i, h) for i in range(length // TILE) for h in range(QUERY_PER_KEY)]

    def products(i, h):
        rows = pl.ds(pl.multiple_of(base + i * TILE, TILE), TILE)
        cols = slice(h * HEAD_SIZE, (h + 1) * HEAD_SIZE)
        qt, gt = q_ref[rows, cols], g_ref[rows, cols]
        own_docs = tile_docs(docs, places + i * (TILE // BLOCK))
        parts = []
        for run in spans(chunk_list(i, length, (piece,))):
            for (_, _, r), (s, dw) in zip(run, run_products(run, piece_ref, qt, gt, after)):
                parts.append((s, dw, bias_rows(docs, first + r // BLOCK, own_docs), r))
        return qt, gt, parts

    seen = set()
    members = []
    ready = products(*steps[0])
    for n, (i, h) in enumerate(steps):
        qt, gt, parts = ready
        if n + 1 < len(steps):
            ready = products(*steps[n + 1])
        lanes = slice(i * TILE, (i + 1) * TILE)
        shift, inverse, row_dot = [stats_ref[h * 3 + k : h * 3 + k + 1, lanes] for k in range(3)]
        weights, dscores = [], []
        for s, dw, bias, r in parts:
            w = chunk_terms(s, bias, shift) * inverse
            dscores.append((w * (dw - row_dot)).astype(jnp.bfloat16))
            weights.append(w.astype(jnp.bfloat16))
        dq_t = dq_part_ref[h * width : (h + 1) * width, lanes] + query_share(
            {piece: key_t}, spans(chunk_list(i, length, (piece,))), dscores
        )
        if piece == 2:
            rows = pl.ds(pl.multiple_of(base + i * TILE, TILE), TILE)
            cols = slice(h * HEAD_SIZE, (h + 1) * HEAD_SIZE)
            dq_ref[rows, cols] = jnp.transpose(dq_t * query_scaling).astype(jnp.bfloat16)
        else:
            dq_ref[h * width : (h + 1) * width, lanes] = dq_t
        members.append((qt, gt, weights, dscores))
        if h == QUERY_PER_KEY - 1:
            slots = [r for _, _, _, r in parts]
            add_key_grads(acc_ref, members, slots, [x for x in slots if x not in seen])
            seen.update(slots)
            members = []


def own_kernel(
    index_ref, q_ref, g_ref, inner_ref, inner_stats, inner_dq, outer_ref, outer_stats, outer_dq,
    dq_ref, inner_out, outer_out,
):
    length = q_ref.shape[0] // 2
    width = inner_ref.shape[1] // 2
    parity = lax.rem(index_ref[0], 2)
    after = triangle()
    for half, own_ref, stats_ref, dq_part_ref, out_ref in (
        (1 - parity, inner_ref, inner_stats, inner_dq, inner_out),
        (parity, outer_ref, outer_stats, outer_dq, outer_out),
    ):
        docs = block_docs((own_ref,), length)
        key_t = jnp.transpose(own_ref[:length, :width])
        piece_share(
            2, 0, half * length, docs, 0, after, key_t, q_ref, g_ref, own_ref,
            stats_ref, dq_part_ref, dq_ref, out_ref,
        )


def fold_kernel(
    last, index_ref, q_ref, g_ref, own_ref, near_ref, far_ref, part_ref,
    near_out, far_out, dq_out, stats_ref, dq_ref, acc_ref,
):
    @pl.when(index_ref[0] == last)
    def _():
        outer_near_kernel(
            index_ref, q_ref, g_ref, own_ref, near_ref, part_ref, near_out, dq_ref, stats_ref,
            acc_ref,
        )
        outer_far_share(
            index_ref, q_ref, g_ref, own_ref, near_ref, far_ref, stats_ref, dq_ref, dq_out, acc_ref
        )
        far_out[...] = acc_ref[...].astype(jnp.bfloat16)


def near_kernel(
    last, index_ref, q_ref, g_ref, own_ref, near_ref, part_ref, fold_near, fold_dq, fold_stats,
    near_out, dq_out, stats_ref, acc_ref,
):
    @pl.when(index_ref[0] != last)
    def _():
        outer_near_kernel(
            index_ref, q_ref, g_ref, own_ref, near_ref, part_ref, near_out, dq_out, stats_ref,
            acc_ref,
        )

    @pl.when(index_ref[0] == last)
    def _():
        near_out[...] = fold_near[...]
        dq_out[...] = fold_dq[...]
        stats_ref[...] = fold_stats[...]


def early_sum_kernel(last, index_ref, own, across, kept, out):
    grad = jnp.where(index_ref[0] == last, kept[...], across[...])
    out[...] = own[...] + grad.astype(jnp.float32)


def sum_kernel(
    index_ref, inner_own, outer_own, pair, first, second, dk_ref, dv_ref, held_ref, sems
):
    length = inner_own.shape[0]
    width = dk_ref.shape[1]
    inner, outer, even = halves(index_ref[0])
    f32 = jnp.float32
    one, two = first[...].astype(f32), second[...].astype(f32)
    copies = []
    for n, half in enumerate((inner, outer)):
        if n == 0:
            total = inner_own[...] + jnp.where(even, two, one)
        else:
            total = outer_own[...] + (pair[...].astype(f32) + jnp.where(even, one, two))
        rows = pl.ds(pl.multiple_of(half * length, length), length)
        for m, out in enumerate((dk_ref, dv_ref)):
            held_ref[2 * n + m] = total[:, m * width : (m + 1) * width].astype(jnp.bfloat16)
            copies.append(
                pltpu.make_async_copy(
                    held_ref.at[2 * n + m], out.at[rows, :], sems.at[2 * n + m]
                )
            )
            copies[-1].start()
    for copy in copies:
        copy.wait()


def smem():
    return pl.BlockSpec(memory_space=pltpu.SMEM)


def hbm():
    return pl.BlockSpec(memory_space=pltpu.HBM)


def vmem():
    return pl.BlockSpec(memory_space=pltpu.VMEM)


LIMIT = pltpu.CompilerParams(vmem_limit_bytes=16 * 1024 * 1024)
SMALL = pltpu.CompilerParams(vmem_limit_bytes=4 * 1024 * 1024)


def on_device(queries, keys, values, grad_out, starts):
    length = keys.shape[0] // 2
    width = keys.shape[1]
    count = lax.axis_size("seq")
    index = lax.axis_index("seq").astype(jnp.int32).reshape(1)
    assert count % 4 == 0
    last = count - 1
    pairs = [(d, d ^ 1) for d in range(count)]
    first = [(d, d ^ 2) for d in range(count)]
    second = [(d, ((d - 2) ^ 2) + 2) for d in range(2, count - 2)]
    across = [(d, d + 1 if d % 2 else d - 1) for d in range(1, last)]
    _, _, even = halves(index[0])

    bf16, f32 = jnp.bfloat16, jnp.float32
    narrow = jax.ShapeDtypeStruct((length, 2 * width), bf16)
    wide = jax.ShapeDtypeStruct((length, 2 * width), f32)
    rows = jax.ShapeDtypeStruct((16, length), f32)
    like_q = jax.ShapeDtypeStruct(queries.shape, bf16)
    unit = 2 * QUERY_PER_KEY * TILE * TILE * width

    def call(kernel, outs, operands, name, work, scratch=(), specs=None, limit=LIMIT, alias=None,
             out_specs=None):
        return pl.pallas_call(
            kernel,
            out_shape=outs,
            in_specs=specs or [smem()] + [vmem()] * (len(operands) - 1),
            out_specs=out_specs or (vmem(),) * len(outs),
            scratch_shapes=list(scratch),
            input_output_aliases=alias or {},
            compiler_params=limit,
            cost_estimate=pl.CostEstimate(
                flops=unit * work, bytes_accessed=1024 * 1024, transcendentals=0
            ),
            name=name,
        )(*operands)

    place = index[0]
    parity = lax.rem(place, 2)
    inner, outer = pack_halves(keys, values, starts, parity, place)
    give_1 = jnp.where(even, outer, inner)
    give_2 = jnp.where(even, inner, outer)

    take_1 = lax.ppermute(give_1, "seq", first)
    heads = lax.axis_size("head")

    def spread(links):
        return [(a * heads + h, b * heads + h) for a, b in links for h in range(heads)]

    fold = [(last - 1, last), (last, last - 1)]
    ends = [(d * heads + h, d * heads + (h ^ 1)) for d in (0, 1) for h in range(heads)]
    take_2 = lax.ppermute(give_2, ("seq", "head"), spread(second + fold) + ends)
    inner_near = lax.ppermute(outer, "seq", pairs)
    inner_far = jnp.where(even, take_1, take_2)
    outer_far = jnp.where(even, take_2, take_1)
    q, g = queries, grad_out
    outer_near = lax.ppermute(inner_far, "seq", pairs)

    def after(value, *others):
        return lax.optimization_barrier((value,) + others)[0]

    grads = pltpu.VMEM((length, 2 * width), f32)
    dq_rows = jax.ShapeDtypeStruct((QUERY_PER_KEY * width, length), f32)

    (part,) = call(
        outer_stats_kernel, (rows,), (index, q, g, outer, outer_far), "outer_stats", 12
    )
    fold_near, fold_far, fold_dq, fold_stats = call(
        lambda *refs: fold_kernel(last, *refs),
        (narrow, narrow, dq_rows, rows),
        (index, q, g, outer, inner, outer_far, part),
        "fold",
        1,
        [pltpu.VMEM(dq_rows.shape, f32), grads],
    )
    inner_g1, inner_g2, inner_dq, inner_stats = call(
        lambda *refs: inner_stage_kernel(last, *refs),
        (narrow, narrow, dq_rows, rows),
        (index, q, g, inner, inner_near, inner_far, fold_far),
        "inner_stage",
        40,
        [pltpu.VMEM((2 * length, 2 * width), f32)],
    )
    pair_take = lax.ppermute(inner_g1, "seq", pairs)
    outer_g1, dq_part, stats = call(
        lambda *refs: near_kernel(last, *refs),
        (narrow, dq_rows, rows),
        (index, after(q, inner_g1), g, outer, outer_near, part, fold_near, fold_dq, fold_stats),
        "outer_near",
        20,
        [grads],
    )
    turns = [(d * heads + h, d * heads + (h ^ 1)) for d in (0, last) for h in range(heads)]
    inner_a = lax.ppermute(outer_g1, ("seq", "head"), spread(across) + turns)
    dq_part, give_1, give_2 = call(
        lambda *refs: outer_far_kernel(last, *refs),
        (dq_rows, narrow, narrow),
        (index, q, g, outer, outer_near, outer_far, stats, dq_part, inner_g2),
        "outer_far",
        15,
        [grads],
    )
    take_1 = lax.ppermute(give_1, "seq", first)
    take_2 = lax.ppermute(give_2, ("seq", "head"), spread(second + fold[:1]) + ends)
    dq, inner_own, outer_own = call(
        own_kernel,
        (like_q, wide, wide),
        (index, q, g, inner, inner_stats, inner_dq, outer, stats, dq_part),
        "own",
        30,
    )
    (inner_own,) = call(
        lambda *refs: early_sum_kernel(last, *refs),
        (wide,),
        (index, inner_own, inner_a, outer_g1),
        "early_sum",
        0,
        limit=SMALL,
    )
    half = jax.ShapeDtypeStruct(keys.shape, bf16)
    dk, dv = call(
        sum_kernel,
        (half, half),
        (index, inner_own, outer_own, pair_take, take_1, take_2),
        "sum",
        1,
        [pltpu.VMEM((4, length, width), bf16), pltpu.SemaphoreType.DMA((4,))],
        limit=SMALL,
        out_specs=(hbm(),) * 2,
    )
    return dq, dk, dv


def solution(mesh):
    in_specs = (P("seq", "head"), P("seq", "head"), P("seq", "head"), P("seq", "head"), P("seq"))
    out_specs = (P("seq", "head"), P("seq", "head"), P("seq", "head"))
    return jax.shard_map(
        on_device, mesh=mesh, in_specs=in_specs, out_specs=out_specs, check_vma=False
    )
```

```python
import math

import jax
import jax.numpy as jnp
from jax import lax
from jax.experimental import pallas as pl
from jax.experimental.pallas import tpu as pltpu
from jax.sharding import PartitionSpec as P

HEAD_SIZE = 128
WINDOW = 1024
QUERY_PER_KEY = 2
BLOCK = 128
TILE = 256
MARK = 16
NEG = -1e30

query_scaling = 168.0 ** (-0.5)
exponent_scale = query_scaling * math.log2(math.e)


def dot(a, b, ca, cb):
    return lax.dot_general(a, b, (((ca,), (cb,)), ((), ())), preferred_element_type=jnp.float32)


def halves(index):
    parity = lax.rem(index, 2)
    even = lax.rem(parity + lax.div(index, 2), 2) == 0
    return 1 - parity, parity, even


def pack_halves(keys, values, starts, parity, place):
    length = keys.shape[0] // 2
    blocks = length // BLOCK
    halves = (1 - parity, parity)
    parts = [
        lax.dynamic_slice_in_dim(x, half * length, length, 0)
        for half in halves
        for x in (keys, values)
    ]
    begins = [starts[:blocks], starts[blocks:]]
    first = (lax.iota(jnp.int32, blocks) == 0) & (place == 0)
    begins[0] = jnp.where(first, 1, begins[0])
    packs = []
    for n, half in enumerate(halves):
        rows = jnp.where(half == 0, begins[0], begins[1]).astype(jnp.bfloat16)
        rows = jnp.pad(rows, (0, MARK - blocks))
        marks = jnp.broadcast_to(rows[:, None], (MARK, 2 * keys.shape[1]))
        both = jnp.concatenate(parts[2 * n : 2 * n + 2], axis=1)
        packs.append(jnp.concatenate([both, marks], axis=0))
    return packs


def block_docs(pieces, length):
    docs = []
    count = jnp.zeros((1, TILE), jnp.float32)
    for piece in pieces:
        marks = piece[length:, :TILE].astype(jnp.float32)
        for j in range(length // BLOCK):
            count = count + marks[j : j + 1, :]
            docs.append(count)
    return docs


def tile_docs(docs, first):
    lane = lax.broadcasted_iota(jnp.int32, (1, TILE), 1)
    own = docs[first]
    for b in range(1, TILE // BLOCK):
        own = jnp.where(lane >= b * BLOCK, docs[first + b], own)
    return own


def chunk_list(tile, length, wanted):
    found = []
    for c in range(WINDOW // TILE + 1):
        piece, row = divmod((tile + c) * TILE, length)
        if piece in wanted:
            found.append((c, piece, row))
    return found


def triangle():
    row = lax.broadcasted_iota(jnp.int32, (TILE, TILE), 0)
    return row > lax.broadcasted_iota(jnp.int32, (TILE, TILE), 1)


def spans(chunks):
    runs = []
    for chunk in chunks:
        if runs and runs[-1][-1][1] == chunk[1]:
            runs[-1].append(chunk)
        else:
            runs.append([chunk])
    return runs


def run_products(run, piece_ref, qt, gt, after):
    width = piece_ref.shape[1] // 2
    rows = slice(run[0][2], run[0][2] + len(run) * TILE)
    scores = dot(piece_ref[rows, :width], qt, 1, 1)
    dweights = dot(piece_ref[rows, width:], gt, 1, 1)
    found = []
    for n, (c, _, _) in enumerate(run):
        s = scores[n * TILE : (n + 1) * TILE]
        if c == 0:
            s = jnp.where(after, s, NEG)
        if c == WINDOW // TILE:
            s = jnp.where(after, NEG, s)
        found.append((s, dweights[n * TILE : (n + 1) * TILE]))
    return found


def query_share(key_t, runs, dscores):
    total = None
    n = 0
    for run in runs:
        p, r = run[0][1:]
        ds = jnp.concatenate(dscores[n : n + len(run)], axis=0)
        n += len(run)
        part = dot(key_t[p][:, r : r + ds.shape[0]], ds, 1, 0)
        total = part if total is None else total + part
    return total


def bias_rows(docs, first, own):
    return [jnp.where(docs[first + b] == own, 0.0, NEG) for b in range(TILE // BLOCK)]


def chunk_top(s, bias, top):
    for b, row in enumerate(bias):
        t = jnp.max(s[b * BLOCK : (b + 1) * BLOCK], axis=0, keepdims=True) + row
        top = t if top is None else jnp.maximum(top, t)
    return top


def chunk_terms(s, bias, shift):
    return jnp.concatenate(
        [
            jnp.exp2(s[b * BLOCK : (b + 1) * BLOCK] * exponent_scale + (row - shift))
            for b, row in enumerate(bias)
        ],
        axis=0,
    )


def softmax_part(parts):
    top = None
    for s, dw, bias in parts:
        top = chunk_top(s, bias, top)
    shift = top * exponent_scale
    total = jnp.zeros((1, TILE), jnp.float32)
    mixed = jnp.zeros((1, TILE), jnp.float32)
    for s, dw, bias in parts:
        e = chunk_terms(s, bias, shift)
        total = total + jnp.sum(e, axis=0, keepdims=True)
        mixed = mixed + jnp.sum(e * dw, axis=0, keepdims=True)
    return top, total, mixed


def outer_stats_kernel(
    index_ref, q_ref, g_ref, own_ref, far_ref, inner_far_ref, stats_ref, far_t_ref, inner_far_t_ref
):
    length = q_ref.shape[0] // 2
    width = own_ref.shape[1] // 2
    far_t_ref[...] = jnp.transpose(far_ref[:length, :width])
    inner_far_t_ref[...] = jnp.transpose(inner_far_ref[:length, :width])
    blocks = length // BLOCK
    base = lax.rem(index_ref[0], 2) * length
    docs = block_docs((far_ref, own_ref), length)
    after = triangle()
    for i in range(length // TILE):
        own_docs = tile_docs(docs, blocks + i * (TILE // BLOCK))
        rows = pl.ds(pl.multiple_of(base + i * TILE, TILE), TILE)
        for h in range(QUERY_PER_KEY):
            cols = slice(h * HEAD_SIZE, (h + 1) * HEAD_SIZE)
            qt, gt = q_ref[rows, cols], g_ref[rows, cols]
            for n, (piece, ref, first) in enumerate(((2, own_ref, blocks), (0, far_ref, 0))):
                parts = []
                for run in spans(chunk_list(i, length, (piece,))):
                    for (_, _, r), (s, dw) in zip(run, run_products(run, ref, qt, gt, after)):
                        parts.append((s, dw, bias_rows(docs, first + r // BLOCK, own_docs)))
                for k, value in enumerate(softmax_part(parts)):
                    at = (h * 2 + n) * 3 + k
                    stats_ref[at : at + 1, i * TILE : (i + 1) * TILE] = value


def outer_near_kernel(
    index_ref, q_ref, g_ref, own_ref, near_ref, part_ref, near_out, dq_out, stats_ref, acc_ref
):
    length = q_ref.shape[0] // 2
    width = own_ref.shape[1] // 2
    blocks = length // BLOCK
    base = lax.rem(index_ref[0], 2) * length
    docs = block_docs((near_ref, own_ref), length)
    far_bias = jnp.where(docs[blocks - 1] == 0.0, 0.0, NEG)
    key_t = jnp.transpose(near_ref[:length, :width])
    steps = [(i, h) for i in range(length // TILE) for h in range(QUERY_PER_KEY)]

    def products(i, h):
        rows = pl.ds(pl.multiple_of(base + i * TILE, TILE), TILE)
        cols = slice(h * HEAD_SIZE, (h + 1) * HEAD_SIZE)
        qt, gt = q_ref[rows, cols], g_ref[rows, cols]
        own_docs = tile_docs(docs, blocks + i * (TILE // BLOCK))
        parts = []
        for run in spans(chunk_list(i, length, (1,))):
            for (_, _, r), (s, dw) in zip(run, run_products(run, near_ref, qt, gt, None)):
                parts.append((s, dw, bias_rows(docs, r // BLOCK, own_docs)))
        return qt, gt, parts

    def shares(i, h, parts):
        lanes = slice(i * TILE, (i + 1) * TILE)
        at = h * 6
        own_top, own_total, own_mixed = [part_ref[at + k : at + k + 1, lanes] for k in range(3)]
        far_top, far_total, far_mixed = [part_ref[at + 3 + k : at + 4 + k, lanes] for k in range(3)]
        top = jnp.maximum(own_top, far_top + far_bias)
        for s, dw, bias in parts:
            top = chunk_top(s, bias, top)
        shift = top * exponent_scale
        own_scale = jnp.exp2(own_top * exponent_scale - shift)
        far_scale = jnp.exp2(far_top * exponent_scale + (far_bias - shift))
        total = own_total * own_scale + far_total * far_scale
        mixed = own_mixed * own_scale + far_mixed * far_scale
        terms = []
        for s, dw, bias in parts:
            e = chunk_terms(s, bias, shift)
            terms.append(e)
            total = total + jnp.sum(e, axis=0, keepdims=True)
            mixed = mixed + jnp.sum(e * dw, axis=0, keepdims=True)
        inverse = 1.0 / total
        row_dot = mixed * inverse
        for k, value in enumerate((shift, inverse, row_dot)):
            stats_ref[h * 3 + k : h * 3 + k + 1, lanes] = value
        weights, dscores = [], []
        for e, (s, dw, bias) in zip(terms, parts):
            w = e * inverse
            dscores.append((w * (dw - row_dot)).astype(jnp.bfloat16))
            weights.append(w.astype(jnp.bfloat16))
        dq_out[h * width : (h + 1) * width, lanes] = query_share(
            {1: key_t}, spans(chunk_list(i, length, (1,))), dscores
        )
        return weights, dscores

    members = []
    ready = products(*steps[0])
    for n, (i, h) in enumerate(steps):
        qt, gt, parts = ready
        if n + 1 < len(steps):
            ready = products(*steps[n + 1])
        members.append((qt, gt, *shares(i, h, parts)))
        if h == QUERY_PER_KEY - 1:
            slots = [r for _, _, r in chunk_list(i, length, (1,))]
            add_key_grads(acc_ref, members, slots, slots if i == 0 else [])
            members = []
    near_out[...] = acc_ref[...].astype(jnp.bfloat16)


def inner_stage_kernel(
    last, index_ref, q_ref, g_ref, own_ref, near_ref, far_ref, fold_ref, far_t_ref,
    near_out, far_out, dq_out, stats_ref, acc_ref,
):
    length = q_ref.shape[0] // 2
    width = own_ref.shape[1] // 2
    blocks = length // BLOCK
    base = (1 - lax.rem(index_ref[0], 2)) * length
    pieces = (far_ref, near_ref, own_ref)
    docs = block_docs(pieces, length)
    after = triangle()
    key_t = [far_t_ref, jnp.transpose(near_ref[:length, :width])]
    steps = [(i, h) for i in range(length // TILE) for h in range(QUERY_PER_KEY)]

    def products(i, h):
        rows = pl.ds(pl.multiple_of(base + i * TILE, TILE), TILE)
        cols = slice(h * HEAD_SIZE, (h + 1) * HEAD_SIZE)
        qt, gt = q_ref[rows, cols], g_ref[rows, cols]
        own_docs = tile_docs(docs, 2 * blocks + i * (TILE // BLOCK))
        parts = []
        for run in spans(chunk_list(i, length, (0, 1, 2))):
            found = run_products(run, pieces[run[0][1]], qt, gt, after)
            for (_, p, r), (s, dw) in zip(run, found):
                parts.append((s, dw, bias_rows(docs, p * blocks + r // BLOCK, own_docs)))
        return qt, gt, parts

    def shares(i, h, parts):
        lanes = slice(i * TILE, (i + 1) * TILE)
        top = None
        for s, dw, bias in parts:
            top = chunk_top(s, bias, top)
        shift = top * exponent_scale
        total = jnp.zeros((1, TILE), jnp.float32)
        mixed = jnp.zeros((1, TILE), jnp.float32)
        terms = []
        for s, dw, bias in parts:
            e = chunk_terms(s, bias, shift)
            terms.append(e)
            total = total + jnp.sum(e, axis=0, keepdims=True)
            mixed = mixed + jnp.sum(e * dw, axis=0, keepdims=True)
        inverse = 1.0 / total
        row_dot = mixed * inverse
        for k, value in enumerate((shift, inverse, row_dot)):
            stats_ref[h * 3 + k : h * 3 + k + 1, lanes] = value
        weights, dscores = [], []
        for e, (s, dw, bias), (c, p, r) in zip(terms, parts, chunk_list(i, length, (0, 1, 2))):
            if p == 2:
                continue
            w = e * inverse
            dscores.append((w * (dw - row_dot)).astype(jnp.bfloat16))
            weights.append(w.astype(jnp.bfloat16))
        dq_out[h * width : (h + 1) * width, lanes] = query_share(
            key_t, spans(chunk_list(i, length, (0, 1))), dscores
        )
        return weights, dscores

    seen = set()
    members = []
    ready = products(*steps[0])
    for n, (i, h) in enumerate(steps):
        qt, gt, parts = ready
        if n + 1 < len(steps):
            ready = products(*steps[n + 1])
        members.append((qt, gt, *shares(i, h, parts)))
        if h == QUERY_PER_KEY - 1:
            slots = [p * length + r for _, p, r in chunk_list(i, length, (0, 1))]
            add_key_grads(acc_ref, members, slots, [x for x in slots if x not in seen])
            seen.update(slots)
            members = []
    more = jnp.where(index_ref[0] == last, fold_ref[...].astype(jnp.float32), 0.0)
    near_out[...] = (acc_ref[length:] + more).astype(jnp.bfloat16)
    far_out[...] = acc_ref[:length].astype(jnp.bfloat16)


def add_key_grads(acc_ref, members, slots, first):
    width = acc_ref.shape[1] // 2
    q_all = jnp.concatenate([m[0] for m in members], axis=0)
    g_all = jnp.concatenate([m[1] for m in members], axis=0)
    n = 0
    while n < len(slots):
        m = n + 1
        while m < len(slots) and slots[m] == slots[m - 1] + TILE and m - n < 2:
            m += 1
        w_all, d_all = [
            jnp.concatenate(
                [jnp.concatenate([x[k][c] for x in members], axis=1) for c in range(n, m)], axis=0
            )
            for k in (2, 3)
        ]
        dk = dot(d_all, q_all, 1, 0) * query_scaling
        dv = dot(w_all, g_all, 1, 0)
        for c in range(n, m):
            at = slice(slots[c], slots[c] + TILE)
            own = slice((c - n) * TILE, (c - n + 1) * TILE)
            if (first is True) or (first is not False and slots[c] in first):
                acc_ref[at, :width] = dk[own]
                acc_ref[at, width:] = dv[own]
            else:
                acc_ref[at, :width] = acc_ref[at, :width] + dk[own]
                acc_ref[at, width:] = acc_ref[at, width:] + dv[own]
        n = m


def outer_far_share(
    index_ref, q_ref, g_ref, own_ref, near_ref, far_ref, stats_ref, dq_part_ref, dq_ref, acc_ref,
    key_t,
):
    length = q_ref.shape[0] // 2
    width = own_ref.shape[1] // 2
    base = lax.rem(index_ref[0], 2) * length
    docs = block_docs((far_ref, near_ref, own_ref), length)
    piece_share(
        0, 0, base, docs, 2 * (length // BLOCK), triangle(), key_t, q_ref, g_ref, far_ref,
        stats_ref, dq_part_ref, dq_ref, acc_ref,
    )


def outer_far_kernel(
    last, index_ref, q_ref, g_ref, own_ref, near_ref, far_ref, stats_ref, dq_part_ref,
    inner_far_ref, far_t_ref, dq_ref, first_out, second_out, acc_ref,
):
    @pl.when(index_ref[0] != last)
    def _():
        outer_far_share(
            index_ref, q_ref, g_ref, own_ref, near_ref, far_ref, stats_ref, dq_part_ref, dq_ref,
            acc_ref, far_t_ref,
        )

    @pl.when(index_ref[0] == last)
    def _():
        dq_ref[...] = dq_part_ref[...]
        acc_ref[...] = jnp.zeros_like(acc_ref)

    _, _, even = halves(index_ref[0])
    grad = acc_ref[...].astype(jnp.bfloat16)
    other = inner_far_ref[...]
    first_out[...] = jnp.where(even, other, grad)
    second_out[...] = jnp.where(even, grad, other)


def piece_share(
    piece, first, base, docs, places, after, key_t, q_ref, g_ref, piece_ref,
    stats_ref, dq_part_ref, dq_ref, acc_ref,
):
    length, width = q_ref.shape[0] // 2, piece_ref.shape[1] // 2
    steps = [(i, h) for i in range(length // TILE) for h in range(QUERY_PER_KEY)]

    def products(i, h):
        rows = pl.ds(pl.multiple_of(base + i * TILE, TILE), TILE)
        cols = slice(h * HEAD_SIZE, (h + 1) * HEAD_SIZE)
        qt, gt = q_ref[rows, cols], g_ref[rows, cols]
        own_docs = tile_docs(docs, places + i * (TILE // BLOCK))
        parts = []
        for run in spans(chunk_list(i, length, (piece,))):
            for (_, _, r), (s, dw) in zip(run, run_products(run, piece_ref, qt, gt, after)):
                parts.append((s, dw, bias_rows(docs, first + r // BLOCK, own_docs), r))
        return qt, gt, parts

    seen = set()
    members = []
    ready = products(*steps[0])
    for n, (i, h) in enumerate(steps):
        qt, gt, parts = ready
        if n + 1 < len(steps):
            ready = products(*steps[n + 1])
        lanes = slice(i * TILE, (i + 1) * TILE)
        shift, inverse, row_dot = [stats_ref[h * 3 + k : h * 3 + k + 1, lanes] for k in range(3)]
        weights, dscores = [], []
        for s, dw, bias, r in parts:
            w = chunk_terms(s, bias, shift) * inverse
            dscores.append((w * (dw - row_dot)).astype(jnp.bfloat16))
            weights.append(w.astype(jnp.bfloat16))
        dq_t = dq_part_ref[h * width : (h + 1) * width, lanes] + query_share(
            {piece: key_t}, spans(chunk_list(i, length, (piece,))), dscores
        )
        if piece == 2:
            rows = pl.ds(pl.multiple_of(base + i * TILE, TILE), TILE)
            cols = slice(h * HEAD_SIZE, (h + 1) * HEAD_SIZE)
            dq_ref[rows, cols] = jnp.transpose(dq_t * query_scaling).astype(jnp.bfloat16)
        else:
            dq_ref[h * width : (h + 1) * width, lanes] = dq_t
        members.append((qt, gt, weights, dscores))
        if h == QUERY_PER_KEY - 1:
            slots = [r for _, _, _, r in parts]
            add_key_grads(acc_ref, members, slots, [x for x in slots if x not in seen])
            seen.update(slots)
            members = []


def own_kernel(
    index_ref, q_ref, g_ref, inner_ref, inner_stats, inner_dq, outer_ref, outer_stats, outer_dq,
    dq_ref, inner_out, outer_out,
):
    length = q_ref.shape[0] // 2
    width = inner_ref.shape[1] // 2
    parity = lax.rem(index_ref[0], 2)
    after = triangle()
    for half, own_ref, stats_ref, dq_part_ref, out_ref in (
        (1 - parity, inner_ref, inner_stats, inner_dq, inner_out),
        (parity, outer_ref, outer_stats, outer_dq, outer_out),
    ):
        docs = block_docs((own_ref,), length)
        key_t = jnp.transpose(own_ref[:length, :width])
        piece_share(
            2, 0, half * length, docs, 0, after, key_t, q_ref, g_ref, own_ref,
            stats_ref, dq_part_ref, dq_ref, out_ref,
        )


def fold_kernel(
    last, index_ref, q_ref, g_ref, own_ref, near_ref, far_ref, part_ref, far_t_ref,
    near_out, far_out, dq_out, stats_ref, dq_ref, acc_ref,
):
    @pl.when(index_ref[0] == last)
    def _():
        outer_near_kernel(
            index_ref, q_ref, g_ref, own_ref, near_ref, part_ref, near_out, dq_ref, stats_ref,
            acc_ref,
        )
        outer_far_share(
            index_ref, q_ref, g_ref, own_ref, near_ref, far_ref, stats_ref, dq_ref, dq_out, acc_ref,
            far_t_ref,
        )
        far_out[...] = acc_ref[...].astype(jnp.bfloat16)


def near_kernel(
    last, index_ref, q_ref, g_ref, own_ref, near_ref, part_ref, fold_near, fold_dq, fold_stats,
    near_out, dq_out, stats_ref, acc_ref,
):
    @pl.when(index_ref[0] != last)
    def _():
        outer_near_kernel(
            index_ref, q_ref, g_ref, own_ref, near_ref, part_ref, near_out, dq_out, stats_ref,
            acc_ref,
        )

    @pl.when(index_ref[0] == last)
    def _():
        near_out[...] = fold_near[...]
        dq_out[...] = fold_dq[...]
        stats_ref[...] = fold_stats[...]


def early_sum_kernel(last, index_ref, own, across, kept, out):
    grad = jnp.where(index_ref[0] == last, kept[...], across[...])
    out[...] = own[...] + grad.astype(jnp.float32)


def sum_kernel(
    index_ref, inner_own, outer_own, pair, first, second, dk_ref, dv_ref, held_ref, sems
):
    length = inner_own.shape[0]
    width = dk_ref.shape[1]
    inner, outer, even = halves(index_ref[0])
    f32 = jnp.float32
    one, two = first[...].astype(f32), second[...].astype(f32)
    copies = []
    for n, half in enumerate((inner, outer)):
        if n == 0:
            total = inner_own[...] + jnp.where(even, two, one)
        else:
            total = outer_own[...] + (pair[...].astype(f32) + jnp.where(even, one, two))
        rows = pl.ds(pl.multiple_of(half * length, length), length)
        for m, out in enumerate((dk_ref, dv_ref)):
            held_ref[2 * n + m] = total[:, m * width : (m + 1) * width].astype(jnp.bfloat16)
            copies.append(
                pltpu.make_async_copy(
                    held_ref.at[2 * n + m], out.at[rows, :], sems.at[2 * n + m]
                )
            )
            copies[-1].start()
    for copy in copies:
        copy.wait()


def smem():
    return pl.BlockSpec(memory_space=pltpu.SMEM)


def hbm():
    return pl.BlockSpec(memory_space=pltpu.HBM)


def vmem():
    return pl.BlockSpec(memory_space=pltpu.VMEM)


LIMIT = pltpu.CompilerParams(vmem_limit_bytes=16 * 1024 * 1024)
SMALL = pltpu.CompilerParams(vmem_limit_bytes=4 * 1024 * 1024)


def on_device(queries, keys, values, grad_out, starts):
    length = keys.shape[0] // 2
    width = keys.shape[1]
    count = lax.axis_size("seq")
    index = lax.axis_index("seq").astype(jnp.int32).reshape(1)
    assert count % 4 == 0
    last = count - 1
    pairs = [(d, d ^ 1) for d in range(count)]
    first = [(d, d ^ 2) for d in range(count)]
    second = [(d, ((d - 2) ^ 2) + 2) for d in range(2, count - 2)]
    across = [(d, d + 1 if d % 2 else d - 1) for d in range(1, last)]
    _, _, even = halves(index[0])

    bf16, f32 = jnp.bfloat16, jnp.float32
    narrow = jax.ShapeDtypeStruct((length, 2 * width), bf16)
    wide = jax.ShapeDtypeStruct((length, 2 * width), f32)
    rows = jax.ShapeDtypeStruct((16, length), f32)
    like_q = jax.ShapeDtypeStruct(queries.shape, bf16)
    unit = 2 * QUERY_PER_KEY * TILE * TILE * width

    def call(kernel, outs, operands, name, work, scratch=(), specs=None, limit=LIMIT, alias=None,
             out_specs=None):
        return pl.pallas_call(
            kernel,
            out_shape=outs,
            in_specs=specs or [smem()] + [vmem()] * (len(operands) - 1),
            out_specs=out_specs or (vmem(),) * len(outs),
            scratch_shapes=list(scratch),
            input_output_aliases=alias or {},
            compiler_params=limit,
            cost_estimate=pl.CostEstimate(
                flops=unit * work, bytes_accessed=1024 * 1024, transcendentals=0
            ),
            name=name,
        )(*operands)

    place = index[0]
    parity = lax.rem(place, 2)
    inner, outer = pack_halves(keys, values, starts, parity, place)
    give_1 = jnp.where(even, outer, inner)
    give_2 = jnp.where(even, inner, outer)

    take_1 = lax.ppermute(give_1, "seq", first)
    heads = lax.axis_size("head")

    def spread(links):
        return [(a * heads + h, b * heads + h) for a, b in links for h in range(heads)]

    fold = [(last - 1, last), (last, last - 1)]
    ends = [(d * heads + h, d * heads + (h ^ 1)) for d in (0, 1) for h in range(heads)]
    take_2 = lax.ppermute(give_2, ("seq", "head"), spread(second + fold) + ends)
    inner_near = lax.ppermute(outer, "seq", pairs)
    inner_far = jnp.where(even, take_1, take_2)
    outer_far = jnp.where(even, take_2, take_1)
    q, g = queries, grad_out
    outer_near = lax.ppermute(inner_far, "seq", pairs)

    def after(value, *others):
        return lax.optimization_barrier((value,) + others)[0]

    grads = pltpu.VMEM((length, 2 * width), f32)
    dq_rows = jax.ShapeDtypeStruct((QUERY_PER_KEY * width, length), f32)

    turned = jax.ShapeDtypeStruct((width, length), bf16)
    part, far_t, inner_far_t = call(
        outer_stats_kernel,
        (rows, turned, turned),
        (index, q, g, outer, outer_far, inner_far),
        "outer_stats",
        12,
    )
    fold_near, fold_far, fold_dq, fold_stats = call(
        lambda *refs: fold_kernel(last, *refs),
        (narrow, narrow, dq_rows, rows),
        (index, q, g, outer, inner, outer_far, part, far_t),
        "fold",
        1,
        [pltpu.VMEM(dq_rows.shape, f32), grads],
    )
    inner_g1, inner_g2, inner_dq, inner_stats = call(
        lambda *refs: inner_stage_kernel(last, *refs),
        (narrow, narrow, dq_rows, rows),
        (index, q, g, inner, inner_near, inner_far, fold_far, inner_far_t),
        "inner_stage",
        40,
        [pltpu.VMEM((2 * length, 2 * width), f32)],
    )
    pair_take = lax.ppermute(inner_g1, "seq", pairs)
    outer_g1, dq_part, stats = call(
        lambda *refs: near_kernel(last, *refs),
        (narrow, dq_rows, rows),
        (index, after(q, inner_g1), g, outer, outer_near, part, fold_near, fold_dq, fold_stats),
        "outer_near",
        20,
        [grads],
    )
    turns = [(d * heads + h, d * heads + (h ^ 1)) for d in (0, last) for h in range(heads)]
    inner_a = lax.ppermute(outer_g1, ("seq", "head"), spread(across) + turns)
    dq_part, give_1, give_2 = call(
        lambda *refs: outer_far_kernel(last, *refs),
        (dq_rows, narrow, narrow),
        (index, q, g, outer, outer_near, outer_far, stats, dq_part, inner_g2, far_t),
        "outer_far",
        15,
        [grads],
    )
    take_1 = lax.ppermute(give_1, "seq", first)
    take_2 = lax.ppermute(give_2, ("seq", "head"), spread(second + fold[:1]) + ends)
    dq, inner_own, outer_own = call(
        own_kernel,
        (like_q, wide, wide),
        (index, q, g, inner, inner_stats, inner_dq, outer, stats, dq_part),
        "own",
        30,
    )
    (inner_own,) = call(
        lambda *refs: early_sum_kernel(last, *refs),
        (wide,),
        (index, inner_own, inner_a, outer_g1),
        "early_sum",
        0,
        limit=SMALL,
    )
    half = jax.ShapeDtypeStruct(keys.shape, bf16)
    dk, dv = call(
        sum_kernel,
        (half, half),
        (index, inner_own, outer_own, pair_take, take_1, take_2),
        "sum",
        1,
        [pltpu.VMEM((4, length, width), bf16), pltpu.SemaphoreType.DMA((4,))],
        limit=SMALL,
        out_specs=(hbm(),) * 2,
    )
    return dq, dk, dv


def solution(mesh):
    in_specs = (P("seq", "head"), P("seq", "head"), P("seq", "head"), P("seq", "head"), P("seq"))
    out_specs = (P("seq", "head"), P("seq", "head"), P("seq", "head"))
    return jax.shard_map(
        on_device, mesh=mesh, in_specs=in_specs, out_specs=out_specs, check_vma=False
    )
```
